256 devices in a mesh: ctx: 32 (over x, z), tp: 8 (over y, core).
Axes of the slice: x: 4, y: 4, z: 8, core: 2. Of those that a mesh axis runs over, the one named last changes fastest.
Arguments:
- doc_lengths: int32 [32], replicated, may hold values from 1 to 1024, 16384 in all
- activations: bfloat16 [16384, 4096], P('ctx'), may hold values from -0.09375 to 0.09375
- queries: bfloat16 [16384, 4096], P('ctx', 'tp'), may hold values from -4.6 to 4.6
- key_heads: bfloat16 [16384, 1024], P('ctx', 'tp'), may hold values from -4.6 to 4.6
- head_values: bfloat16 [16384, 1024], P('ctx', 'tp'), may hold values from -6 to 6
- output_gradient: bfloat16 [16384, 4096], P('ctx', 'tp'), may hold values from -6 to 6
Outputs:
- query_weight_grad: bfloat16 [4096, 4096], P('ctx', 'tp')
- key_weight_grad: bfloat16 [4096, 1024], P('ctx', 'tp')
- value_weight_grad: bfloat16 [4096, 1024], P('ctx', 'tp')
The draws below stay inside these ranges and needn't reach their ends.
Inputs may be any that keep to these rules, and one draw needn't show every extreme that they name: `doc_lengths`: the lengths sum to 16384; the longest document has exactly 1024 tokens.
All inputs are finite; a program needn't handle non-finite values.
Results may differ from the reference program's by a relative error of at most 0.025.
Values may be sent and summed in bfloat16 or wider, within the bound.
A program may use at most 64 MiB of HBM per device.

```python
import math
import jax
import jax.numpy as jnp
import numpy as np
from jax import lax

D = 4096
QUERY_HEADS = 32
KEY_VALUE_HEADS = 8
HEAD_SIZE = 128
TOKENS_PER_SLICE = 512
SPAN = 2
PACKED_TOKENS = 16384
MAXDOC = 1024
NDOCS = 32
N_CTX = 32


def draw_queries(key, part):
    key = jax.random.fold_in(key, 1)
    final_result = jnp.clip(jax.random.normal(key, (PACKED_TOKENS, QUERY_HEADS * HEAD_SIZE)), -4.0, 4.0)
    return final_result.astype(jnp.bfloat16)


def draw_key_heads(key, part):
    key = jax.random.fold_in(key, 2)
    final_result = jnp.clip(jax.random.normal(key, (PACKED_TOKENS, KEY_VALUE_HEADS * HEAD_SIZE)), -4.0, 4.0)
    return final_result.astype(jnp.bfloat16)


def spiked(drawn, own_key, source, target, shards_of, factor):
    def block_of(position):
        return (jnp.arange(drawn.shape[position]) // (drawn.shape[position] // shards_of)).reshape((-1,) + (1,) * (drawn.ndim - 1 - position))

    first = jax.random.permutation(own_key, shards_of)[block_of(target)]
    other_side = (block_of(target) + shards_of // 2) % shards_of
    return jnp.where((block_of(source) == first) | (block_of(source) == other_side), factor * drawn, drawn)


def steps_of(rng, extent, split, smallest, high):
    level = 1.0
    for dim, shards_of in split:
        draws = jax.random.uniform(jax.random.fold_in(jax.random.fold_in(rng, 6), dim), (shards_of,), jnp.float32, smallest / len(split), high / len(split))
        level = level * jnp.repeat(jnp.exp(draws), extent[dim] // shards_of).reshape((-1,) + (1,) * (len(extent) - 1 - dim))
    return level


def split_up(number_of, total, reach, skew):
    loads = [(1 << 20) // math.isqrt(grade ** skew) + 1 for grade in range(2, number_of + 1)]
    spare, counts = total - reach - (number_of - 1), [1] * (number_of - 1)
    while spare > 0:
        candidates = [i for i in range(number_of - 1) if counts[i] < reach]
        whole, remaining = sum([loads[i] for i in candidates]), spare
        for i in candidates:
            addition = min(reach - counts[i], max(1, remaining * loads[i] // whole), spare)
            counts[i] = counts[i] + addition
            spare = spare - addition
    return np.array([reach] + counts)


def ragged_sizes(own_key, number_of, total, most, slope):
    if number_of == 2:
        one = jax.random.randint(own_key, (), max(1, total - most), min(most, total - 1) + 1)
        return jnp.stack([one, total - one])
    lengths = jnp.asarray(split_up(number_of, total, most, slope), jnp.int32)
    pairs = (number_of - 1) // 2
    donor, receiver = lengths[1:1 + 2 * pairs:2], lengths[2:2 + 2 * pairs:2]
    room = jnp.minimum(donor - 1, most - receiver)
    moved = jax.random.randint(jax.random.fold_in(own_key, 1), (pairs,), 0, 1 << 20) % (room + 1)
    lengths = lengths.at[1:1 + 2 * pairs:2].set(donor - moved).at[2:2 + 2 * pairs:2].set(receiver + moved)
    return lengths[jax.random.permutation(jax.random.fold_in(own_key, 2), number_of)]


def scatter_about(rng, extent, deviation, bound, split=(), kind=jnp.bfloat16):
    gain = steps_of(rng, extent, split, -0.22, 0.18) if split else 1.0
    values = jax.random.normal(rng, extent, jnp.float32) * deviation * gain
    return jnp.minimum(jnp.maximum(values, -bound), bound).astype(kind)


def gaussian_with(key, dims, scale, most, pieces, heavy, kind=jnp.bfloat16):
    drawn = scale * jax.random.normal(key, dims, jnp.float32)
    if pieces:
        drawn = drawn * steps_of(key, dims, pieces, -0.22, 0.18)
    return jnp.clip(spiked(drawn, jax.random.fold_in(key, 3), *heavy), -most, most).astype(kind)


def setup_inputs(seed: int = 0) -> dict:
    streams_of = jax.random.split(jax.random.key(seed), 7)
    doc_lengths = ragged_sizes(streams_of[0], NDOCS, PACKED_TOKENS, MAXDOC, 2).astype(jnp.int32)
    activations = gaussian_with(streams_of[1], (PACKED_TOKENS, D), PACKED_TOKENS ** -0.5, 0.09375, ((0, 32),), (0, 1, 32, 2.75))
    queries = draw_queries(jax.random.fold_in(streams_of[6], 71), 0)
    key_heads = draw_key_heads(jax.random.fold_in(streams_of[6], 71), 0)
    head_values = scatter_about(streams_of[4], (PACKED_TOKENS, KEY_VALUE_HEADS * HEAD_SIZE), 1.0, 6.0, ((0, 32), (1, 8)))
    output_gradient = scatter_about(streams_of[5], (PACKED_TOKENS, QUERY_HEADS * HEAD_SIZE), 1.0, 6.0, ((0, 32), (1, 8)))
    return dict(doc_lengths=doc_lengths, activations=activations, queries=queries, key_heads=key_heads, head_values=head_values, output_gradient=output_gradient)


def doc_index(doc_ends, positions):
    return lax.optimization_barrier(jnp.sum((doc_ends[None, :] <= positions[:, None]).astype(jnp.int32), axis=1))

def weight_grad(activations, grads):

    def add_shard(total, shard):
        leading_row = (shard * TOKENS_PER_SLICE).astype(jnp.int32)
        block_acts = lax.dynamic_slice_in_dim(activations, leading_row, TOKENS_PER_SLICE, 0)
        block_grads = lax.dynamic_slice_in_dim(grads, leading_row, TOKENS_PER_SLICE, 0)
        partial_sum = jnp.dot(block_acts.T, block_grads, preferred_element_type=jnp.float32)
        rounded = lax.optimization_barrier(partial_sum.astype(jnp.bfloat16))
        return (total + rounded.astype(jnp.float32), None)
    start_total = jnp.zeros((activations.shape[1], grads.shape[1]), jnp.float32)
    total, ignored = lax.scan(add_shard, start_total, jnp.arange(N_CTX, dtype=jnp.int32))
    return total.astype(jnp.bfloat16)

def reference(doc_lengths, activations, queries, key_heads, head_values, output_gradient):
    query_group_size = QUERY_HEADS // KEY_VALUE_HEADS
    att_scale = HEAD_SIZE ** (-0.5)
    key_value_width = KEY_VALUE_HEADS * HEAD_SIZE
    margin = SPAN * TOKENS_PER_SLICE
    span_rows = margin + TOKENS_PER_SLICE
    padded_keys = jnp.concatenate([jnp.zeros((margin, key_value_width), key_heads.dtype), key_heads], 0)
    padded_values = jnp.concatenate([jnp.zeros((margin, key_value_width), head_values.dtype), head_values], 0)
    doc_ends = jnp.cumsum(doc_lengths).astype(jnp.int32)

    def block_grads(carry, shard):
        key_total, value_total = carry
        leading_row = (shard * TOKENS_PER_SLICE).astype(jnp.int32)
        query_tile_rows = lax.dynamic_slice_in_dim(queries, leading_row, TOKENS_PER_SLICE, 0).astype(jnp.float32).reshape(TOKENS_PER_SLICE, KEY_VALUE_HEADS, query_group_size, HEAD_SIZE)
        gradient_block = lax.dynamic_slice_in_dim(output_gradient, leading_row, TOKENS_PER_SLICE, 0).astype(jnp.float32).reshape(TOKENS_PER_SLICE, KEY_VALUE_HEADS, query_group_size, HEAD_SIZE)
        key_span_rows = lax.dynamic_slice_in_dim(padded_keys, leading_row, span_rows, 0).astype(jnp.float32).reshape(span_rows, KEY_VALUE_HEADS, HEAD_SIZE)
        value_span_rows = lax.dynamic_slice_in_dim(padded_values, leading_row, span_rows, 0).astype(jnp.float32).reshape(span_rows, KEY_VALUE_HEADS, HEAD_SIZE)
        query_pos = leading_row + jnp.arange(TOKENS_PER_SLICE, dtype=jnp.int32)
        key_pos = leading_row - margin + jnp.arange(span_rows, dtype=jnp.int32)
        same_doc = doc_index(doc_ends, query_pos)[:, None] == doc_index(doc_ends, key_pos)[None, :]
        visible = same_doc & (key_pos[None, :] <= query_pos[:, None]) & (key_pos[None, :] >= 0)
        scores = jnp.einsum('tngd,knd->ngtk', query_tile_rows, key_span_rows) * att_scale
        scores = jnp.where(visible[None, None], scores, -jnp.inf)
        row_max = lax.optimization_barrier(jnp.max(scores, axis=-1, keepdims=True))
        weights = jnp.exp(scores - row_max)
        probs = weights / lax.optimization_barrier(jnp.sum(weights, axis=-1, keepdims=True))
        probs_low = lax.optimization_barrier(probs.astype(jnp.bfloat16)).astype(jnp.float32)
        attended = jnp.einsum('ngtk,knd->ngtd', probs_low, value_span_rows)
        delta = lax.optimization_barrier(jnp.sum(jnp.transpose(gradient_block, (1, 2, 0, 3)) * attended, axis=-1))
        dprobs = jnp.einsum('tngd,knd->ngtk', gradient_block, value_span_rows)
        dscores = probs * (dprobs - delta[..., None])
        dscores_low = lax.optimization_barrier(dscores.astype(jnp.bfloat16)).astype(jnp.float32)
        query_grad = jnp.einsum('ngtk,knd->tngd', dscores_low, key_span_rows) * att_scale
        key_grad = jnp.einsum('ngtk,tngd->knd', dscores_low, query_tile_rows) * att_scale
        value_grad = jnp.einsum('ngtk,tngd->knd', probs_low, gradient_block)
        key_now = lax.dynamic_slice_in_dim(key_total, leading_row, span_rows, 0)
        key_total = lax.dynamic_update_slice_in_dim(key_total, key_now + key_grad.reshape(span_rows, key_value_width), leading_row, 0)
        value_now = lax.dynamic_slice_in_dim(value_total, leading_row, span_rows, 0)
        value_total = lax.dynamic_update_slice_in_dim(value_total, value_now + value_grad.reshape(span_rows, key_value_width), leading_row, 0)
        return ((key_total, value_total), query_grad.reshape(TOKENS_PER_SLICE, QUERY_HEADS * HEAD_SIZE))
    empty = jnp.zeros((margin + PACKED_TOKENS, key_value_width), jnp.float32)
    totals, query_blocks = lax.scan(block_grads, (empty, empty), jnp.arange(N_CTX, dtype=jnp.int32))
    query_grad = query_blocks.reshape(PACKED_TOKENS, QUERY_HEADS * HEAD_SIZE).astype(jnp.bfloat16)
    key_grad = totals[0][margin:].astype(jnp.bfloat16)
    value_grad = totals[1][margin:].astype(jnp.bfloat16)
    return (weight_grad(activations, query_grad), weight_grad(activations, key_grad), weight_grad(activations, value_grad))
```

```python
import functools

import jax
import jax.numpy as jnp
from jax import lax
from jax.experimental import pallas as pl
from jax.experimental.pallas import tpu as pltpu
from jax.sharding import PartitionSpec as P

HEAD_SIZE = 128
SPAN = 2
NX, NZ = 4, 8
NY, NCORE = 4, 2
GROUPS = 3
WIDE = 256
MESH = pl.DeviceIdType.MESH


def passed_along(value, axis, steps):
    count = lax.axis_size(axis)
    initial, last = (max(0, -steps), min(count, count - steps))
    return lax.ppermute(value, axis, [(source, source + steps) for source in range(initial, last)])


def doc_index(doc_ends, positions):
    return jnp.sum((doc_ends[None, :] <= positions[:, None]).astype(jnp.int32), axis=1)


class Place:
    def __init__(self):
        self.c = lax.axis_index("ctx")
        self.t = lax.axis_index("tp")
        self.x = lax.div(self.c, NZ)
        self.z = lax.rem(self.c, NZ)
        self.y = lax.div(self.t, NCORE)
        self.core = lax.rem(self.t, NCORE)

    def at_x(self, step):
        return (lax.rem(self.x + step + NX, NX) * NZ + self.z, self.t)

    def at_z(self, step):
        return (self.x * NZ + lax.rem(self.z + step + NZ, NZ), self.t)

    def at_y(self, step):
        return (self.c, lax.rem(self.y + step + NY, NY) * NCORE + self.core)

    def sibling(self):
        return (self.c, self.y * NCORE + 1 - self.core)

    def part(self, ystep, other_core):
        core = 1 - self.core if other_core else self.core
        return lax.rem(self.y + ystep + NY, NY) * NCORE + core


def remote(src, dst, send, recv, device):
    return pltpu.make_async_remote_copy(
        src_ref=src, dst_ref=dst, send_sem=send, recv_sem=recv, device_id=device, device_id_type=MESH
    )


class Acts:
    def __init__(self, place, act, abuf, local, sends, recvs):
        self.p, self.act, self.abuf, self.local, self.sends, self.recvs = place, act, abuf, local, sends, recvs
        self.tokens = act.shape[0]
        self.share = self.tokens // (NY * NCORE)
        self.quarter = act.shape[1] // NX

    def rows(self, part):
        return pl.ds(pl.multiple_of(part * self.share, self.share), self.share)

    def own(self):
        cols = pl.ds(pl.multiple_of(self.p.x * self.quarter, self.quarter), self.quarter)
        return pltpu.make_async_copy(self.act.at[:, cols], self.abuf.at[0], self.local)

    def x_copy(self, step):
        there = lax.rem(self.p.x + step, NX)
        cols = pl.ds(pl.multiple_of(there * self.quarter, self.quarter), self.quarter)
        rows = self.rows(self.p.t)
        return remote(
            self.act.at[rows, cols],
            self.abuf.at[step, rows, :],
            self.sends.at[step - 1],
            self.recvs.at[step - 1],
            self.p.at_x(step),
        )

    def y_copy(self, step):
        rows = self.rows(self.p.t)
        piece = self.abuf.at[pl.ds(1, NX - 1), rows, :]
        return remote(piece, piece, self.sends.at[2 + step], self.recvs.at[2 + step], self.p.at_y(step))

    def y_landed(self, step):
        rows = self.rows(self.p.part(-step, False))
        piece = self.abuf.at[pl.ds(1, NX - 1), rows, :]
        return remote(piece, piece, self.sends.at[2 + step], self.recvs.at[2 + step], self.p.at_y(step))

    def core_copy(self, step):
        rows = self.rows(self.p.part(-step, False))
        piece = self.abuf.at[pl.ds(1, NX - 1), rows, :]
        return remote(piece, piece, self.sends.at[6 + step], self.recvs.at[6 + step], self.p.sibling())

    def start(self):
        self.own().start()
        for step in (2, 1, 3):
            self.x_copy(step).start()

    def spread_y(self):
        for step in (1, 2, 3):
            self.x_copy(step).wait_recv()
        for step in (2, 1, 3):
            self.y_copy(step).start()
        self.core_copy(0).start()

    def spread_core(self):
        for step in (1, 3, 2):
            self.y_landed(step).wait_recv()
            self.core_copy(step).start()

    def landed(self):
        self.own().wait()
        for step in range(NY):
            self.core_copy(step).wait_recv()

    def finish(self):
        for step in (1, 2, 3):
            self.x_copy(step).wait_send()
            self.y_copy(step).wait_send()
        for step in range(NY):
            self.core_copy(step).wait_send()


class Gather:
    def __init__(self, place, gbuf, sends, recvs):
        self.p, self.gbuf, self.sends, self.recvs = place, gbuf, sends, recvs

    def copy(self, group, way):
        whole = pl.ds(group * WIDE, WIDE)
        half = WIDE // 2
        source, target, rows, step = (
            (0, 1, whole, 1),
            (0, 3, whole, -1),
            (1, 2, pl.ds(group * WIDE, half), 1),
            (3, 2, pl.ds(group * WIDE + half, half), -1),
        )[way]
        return remote(
            self.gbuf.at[source, rows, :],
            self.gbuf.at[target, rows, :],
            self.sends.at[group, way],
            self.recvs.at[group, way],
            self.p.at_x(step),
        )

    def start(self, group):
        self.copy(group, 0).start()
        self.copy(group, 1).start()

    def forward(self, group):
        self.copy(group, 0).wait_recv()
        self.copy(group, 2).start()
        self.copy(group, 1).wait_recv()
        self.copy(group, 3).start()

    def landed(self, group):
        self.copy(group, 2).wait_recv()
        self.copy(group, 3).wait_recv()

    def finish(self, group):
        for way in range(4):
            self.copy(group, way).wait_send()


class Scatter:
    def __init__(self, place, terms, sbuf, rbuf, sends, recvs):
        self.p, self.terms, self.sbuf, self.rbuf, self.sends, self.recvs = place, terms, sbuf, rbuf, sends, recvs

    def rows(self, way, step):
        if step:
            return slice(0, WIDE)
        return slice(way * (WIDE // 2), (way + 1) * (WIDE // 2))

    def copy(self, group, way, step):
        rows = self.rows(way, step)
        return remote(
            self.sbuf.at[group, way, step, rows, :],
            self.rbuf.at[group, way, step, rows, :],
            self.sends.at[group, way, step],
            self.recvs.at[group, way, step],
            self.p.at_z(1 - 2 * way),
        )

    def step(self, group, step):
        for way in range(2):
            owner = lax.rem(self.p.z + (1 - 2 * way) * (NZ // 2 - step) + NZ, NZ)
            if step:
                self.copy(group, way, step - 1).wait_recv()
            for half in range(2):
                rows = slice(half * (WIDE // 2), (half + 1) * (WIDE // 2))
                if step == 0 and half != way:
                    continue
                total = self.terms[group, owner, rows, :]
                if step > 1 or (step == 1 and half == way):
                    total += self.rbuf[group, way, step - 1, rows, :].astype(jnp.float32)
                self.sbuf[group, way, step, rows, :] = total.astype(jnp.bfloat16)
            self.copy(group, way, step).start()

    def result(self, group):
        last = NZ // 2 - 1
        total = self.terms[group, self.p.z]
        for way in range(2):
            self.copy(group, way, last).wait_recv()
            total += self.rbuf[group, way, last].astype(jnp.float32)
        return total.T.astype(jnp.bfloat16)

    def finish(self, group):
        for way in range(2):
            for step in range(NZ // 2):
                self.copy(group, way, step).wait_send()


def weight_terms(group, abuf, gbuf, terms):
    rows = pl.ds(group * WIDE, WIDE)
    width = terms.shape[3]
    per = WIDE // width

    def columns(n, carry):
        cols = pl.ds(pl.multiple_of(n * WIDE, WIDE), WIDE)
        total = None
        for slot in range(NX):
            term = jnp.dot(gbuf[slot, rows, :], abuf[slot, :, cols], preferred_element_type=jnp.float32)
            total = term if total is None else total + term
        for k in range(per):
            terms[group, n * per + k] = total[:, k * width : (k + 1) * width]
        return carry

    lax.fori_loop(0, NZ // per, columns, 0)


def greet(place):
    barrier = pltpu.get_barrier_semaphore()
    others = [place.at_x(s) for s in (1, 2, 3)] + [place.at_y(s) for s in (1, 2, 3)]
    others += [place.sibling(), place.at_z(1), place.at_z(-1)]
    for other in others:
        pl.semaphore_signal(barrier, inc=1, device_id=other, device_id_type=MESH)
    pl.semaphore_wait(barrier, len(others))


def weights_kernel(
    act, grads, wq, wk, wv, abuf, gbuf, terms, sbuf, rbuf, local, own_sem, as_, ar_, gs_, gr_, ss_, sr_
):
    place = Place()
    acts = Acts(place, act, abuf, local, as_, ar_)
    gather = Gather(place, gbuf, gs_, gr_)
    scatter = Scatter(place, terms, sbuf, rbuf, ss_, sr_)
    own = pltpu.make_async_copy(grads, gbuf.at[0], own_sem)
    own.start()
    greet(place)
    acts.start()
    own.wait()
    for group in range(GROUPS):
        gather.start(group)
    acts.spread_y()
    gather.forward(0)
    gather.forward(1)
    acts.spread_core()
    gather.forward(2)
    acts.landed()
    order = [(0, 0)], [(0, 1), (1, 0)], [(0, 2), (1, 1), (2, 0)]
    for group in range(GROUPS):
        gather.landed(group)
        weight_terms(group, abuf, gbuf, terms)
        for which, step in order[group]:
            scatter.step(which, step)
    for which, step in [(0, 3), (1, 2), (2, 1), (1, 3), (2, 2)]:
        scatter.step(which, step)
    wq[:, 0:WIDE] = scatter.result(0)
    scatter.step(2, 3)
    wq[:, WIDE : 2 * WIDE] = scatter.result(1)
    both = scatter.result(2)
    wk[...] = both[:, 0:HEAD_SIZE]
    wv[...] = both[:, HEAD_SIZE:WIDE]
    acts.finish()
    for group in range(GROUPS):
        gather.finish(group)
        scatter.finish(group)


def weight_grads(activations, grads):
    tokens, features = activations.shape
    quarter = features // NX
    chunk = quarter // NZ
    bf16, f32 = jnp.bfloat16, jnp.float32
    dma = pltpu.SemaphoreType.DMA
    return pl.pallas_call(
        weights_kernel,
        out_shape=(
            jax.ShapeDtypeStruct((chunk, 2 * WIDE), bf16),
            jax.ShapeDtypeStruct((chunk, HEAD_SIZE), bf16),
            jax.ShapeDtypeStruct((chunk, HEAD_SIZE), bf16),
        ),
        in_specs=[pl.BlockSpec(memory_space=pl.ANY), pl.BlockSpec(memory_space=pl.ANY)],
        out_specs=[pl.BlockSpec(memory_space=pltpu.VMEM)] * 3,
        scratch_shapes=[
            pltpu.VMEM((NX, tokens, quarter), bf16),
            pltpu.VMEM((NX, GROUPS * WIDE, tokens), bf16),
            pltpu.VMEM((GROUPS, NZ, WIDE, chunk), f32),
            pltpu.VMEM((GROUPS, 2, NZ // 2, WIDE, chunk), bf16),
            pltpu.VMEM((GROUPS, 2, NZ // 2, WIDE, chunk), bf16),
            dma,
            dma,
            dma((10,)),
            dma((10,)),
            dma((GROUPS, 4)),
            dma((GROUPS, 4)),
            dma((GROUPS, 2, NZ // 2)),
            dma((GROUPS, 2, NZ // 2)),
        ],
        compiler_params=pltpu.CompilerParams(
            collective_id=0, has_side_effects=True, vmem_limit_bytes=40 * 2**20
        ),
    )(activations, grads)


def shards(doc_lengths, activations, queries, key_heads, head_values, output_gradient):
    tok_rows = key_heads.shape[0]
    key_value_width = key_heads.shape[1]
    query_group_size = queries.shape[1] // key_value_width
    group_width = query_group_size * HEAD_SIZE
    att_scale = HEAD_SIZE ** (-0.5)
    first_pos = lax.axis_index("ctx") * tok_rows
    docs = jnp.arange(doc_lengths.shape[0])
    doc_ends = jnp.sum(jnp.where(docs[None, :] <= docs[:, None], doc_lengths[None, :], 0), axis=1)
    query_pos = first_pos + jnp.arange(tok_rows, dtype=jnp.int32)
    key_pos = first_pos - SPAN * tok_rows + jnp.arange((SPAN + 1) * tok_rows, dtype=jnp.int32)
    same_doc = doc_index(doc_ends, query_pos)[:, None] == doc_index(doc_ends, key_pos)[None, :]
    visible = same_doc & (key_pos[None, :] <= query_pos[:, None]) & (key_pos[None, :] >= 0)
    packed = jnp.concatenate([key_heads, head_values], axis=1)
    gone = [passed_along(packed, "ctx", distance) for distance in range(1, SPAN + 1)]
    span_rows = jnp.concatenate(gone[::-1] + [packed], axis=0)
    key_span_rows = span_rows[:, :key_value_width]
    value_span_rows = span_rows[:, key_value_width:]
    query_group = queries.reshape(tok_rows, query_group_size, HEAD_SIZE)
    grad_group = output_gradient.reshape(tok_rows, query_group_size, HEAD_SIZE)
    scores = (
        jnp.einsum("tgd,kd->gtk", query_group, key_span_rows, preferred_element_type=jnp.float32)
        * att_scale
    )
    scores = jnp.where(visible[None], scores, -jnp.inf)
    row_max = jnp.max(scores, axis=-1, keepdims=True)
    weights = jnp.exp(scores - row_max)
    probs = weights / jnp.sum(weights, axis=-1, keepdims=True)
    probs_low = probs.astype(jnp.bfloat16)
    attended = jnp.einsum(
        "gtk,kd->gtd", probs_low, value_span_rows, preferred_element_type=jnp.float32
    )
    delta = jnp.sum(jnp.transpose(grad_group, (1, 0, 2)).astype(jnp.float32) * attended, axis=-1)
    dprobs = jnp.einsum(
        "tgd,kd->gtk", grad_group, value_span_rows, preferred_element_type=jnp.float32
    )
    dscores = probs * (dprobs - delta[..., None])
    dscores_low = dscores.astype(jnp.bfloat16)
    query_grad = (
        jnp.einsum("gtk,kd->tgd", dscores_low, key_span_rows, preferred_element_type=jnp.float32)
        * att_scale
    )
    key_grad = (
        jnp.einsum("gtk,tgd->kd", dscores_low, query_group, preferred_element_type=jnp.float32)
        * att_scale
    )
    value_grad = jnp.einsum(
        "gtk,tgd->kd", probs_low, grad_group, preferred_element_type=jnp.float32
    )
    query_low = query_grad.reshape(tok_rows, group_width).astype(jnp.bfloat16)
    kv_grad = jnp.concatenate([key_grad, value_grad], axis=1)
    far_terms = [
        kv_grad[(SPAN - 1 - offset) * tok_rows : (SPAN - offset) * tok_rows]
        for offset in range(SPAN)
    ]
    returned = kv_grad[SPAN * tok_rows :]
    for distance in range(1, SPAN + 1):
        returned = returned + passed_along(
            far_terms[distance - 1].astype(jnp.bfloat16), "ctx", -distance
        ).astype(jnp.float32)
    kv_low = returned.astype(jnp.bfloat16)
    joined = jnp.concatenate([query_low, kv_low], axis=1)
    return weight_grads(activations, joined.T)


def solution(mesh):
    return jax.shard_map(
        shards,
        mesh=mesh,
        in_specs=(
            P(),
            P("ctx", None),
            P("ctx", "tp"),
            P("ctx", "tp"),
            P("ctx", "tp"),
            P("ctx", "tp"),
        ),
        out_specs=(P("ctx", "tp"), P("ctx", "tp"), P("ctx", "tp")),
        check_vma=False,
    )
```

```python
import math

import jax
import jax.numpy as jnp
from jax import lax
from jax.experimental import pallas as pl
from jax.experimental.pallas import tpu as pltpu
from jax.sharding import PartitionSpec as P

HEAD_SIZE = 128
SPAN = 2
NX, NZ = 4, 8
NY, NCORE = 4, 2
GROUPS = 3
WIDE = 256
REACH = 5
MESH = pl.DeviceIdType.MESH


class Place:
    def __init__(self):
        self.c = lax.axis_index("ctx")
        self.t = lax.axis_index("tp")
        self.x = lax.div(self.c, NZ)
        self.z = lax.rem(self.c, NZ)
        self.y = lax.div(self.t, NCORE)
        self.core = lax.rem(self.t, NCORE)

    def at_x(self, step):
        return (lax.rem(self.x + step + NX, NX) * NZ + self.z, self.t)

    def at_z(self, step):
        return (self.x * NZ + lax.rem(self.z + step + NZ, NZ), self.t)

    def at_y(self, step):
        return (self.c, lax.rem(self.y + step + NY, NY) * NCORE + self.core)

    def at_c(self, step):
        count = NX * NZ
        return (lax.rem(self.c + step + count, count), self.t)

    def sibling(self):
        return (self.c, self.y * NCORE + 1 - self.core)

    def part(self, ystep, other_core):
        core = 1 - self.core if other_core else self.core
        return lax.rem(self.y + ystep + NY, NY) * NCORE + core


def remote(src, dst, send, recv, device):
    return pltpu.make_async_remote_copy(
        src_ref=src, dst_ref=dst, send_sem=send, recv_sem=recv, device_id=device, device_id_type=MESH
    )


class Acts:
    def __init__(self, place, act, abuf, local, sends, recvs):
        self.p, self.act, self.abuf, self.local, self.sends, self.recvs = place, act, abuf, local, sends, recvs
        self.tokens = act.shape[0]
        self.share = self.tokens // (NY * NCORE)
        self.quarter = act.shape[1] // NX

    def rows(self, part):
        return pl.ds(pl.multiple_of(part * self.share, self.share), self.share)

    def own(self):
        cols = pl.ds(pl.multiple_of(self.p.x * self.quarter, self.quarter), self.quarter)
        return pltpu.make_async_copy(self.act.at[:, cols], self.abuf.at[0], self.local)

    def x_copy(self, step):
        there = lax.rem(self.p.x + step, NX)
        cols = pl.ds(pl.multiple_of(there * self.quarter, self.quarter), self.quarter)
        rows = self.rows(self.p.t)
        return remote(
            self.act.at[rows, cols],
            self.abuf.at[step, rows, :],
            self.sends.at[step - 1],
            self.recvs.at[step - 1],
            self.p.at_x(step),
        )

    def y_copy(self, step):
        rows = self.rows(self.p.t)
        piece = self.abuf.at[pl.ds(1, NX - 1), rows, :]
        return remote(piece, piece, self.sends.at[2 + step], self.recvs.at[2 + step], self.p.at_y(step))

    def y_landed(self, step):
        rows = self.rows(self.p.part(-step, False))
        piece = self.abuf.at[pl.ds(1, NX - 1), rows, :]
        return remote(piece, piece, self.sends.at[2 + step], self.recvs.at[2 + step], self.p.at_y(step))

    def core_copy(self, step):
        rows = self.rows(self.p.part(-step, False))
        piece = self.abuf.at[pl.ds(1, NX - 1), rows, :]
        return remote(piece, piece, self.sends.at[6 + step], self.recvs.at[6 + step], self.p.sibling())

    def start(self):
        self.own().start()
        for step in (2, 1, 3):
            self.x_copy(step).start()

    def spread_y(self):
        for step in (1, 2, 3):
            self.x_copy(step).wait_recv()
        for step in (2, 1, 3):
            self.y_copy(step).start()
        self.core_copy(0).start()

    def spread_core(self):
        for step in (1, 3, 2):
            self.y_landed(step).wait_recv()
            self.core_copy(step).start()

    def landed(self):
        self.own().wait()
        for step in range(NY):
            self.core_copy(step).wait_recv()

    def finish(self):
        for step in (1, 2, 3):
            self.x_copy(step).wait_send()
            self.y_copy(step).wait_send()
        for step in range(NY):
            self.core_copy(step).wait_send()


class Gather:
    def __init__(self, place, gbuf, sends, recvs):
        self.p, self.gbuf, self.sends, self.recvs = place, gbuf, sends, recvs

    def copy(self, group, way):
        whole = pl.ds(pl.multiple_of(group * HEAD_SIZE, HEAD_SIZE), HEAD_SIZE)
        half = HEAD_SIZE // 2
        lower = pl.ds(pl.multiple_of(group * HEAD_SIZE, half), half)
        upper = pl.ds(pl.multiple_of(group * HEAD_SIZE + half, half), half)
        source, target, rows, step = (
            (0, 1, whole, 1),
            (0, 3, whole, -1),
            (1, 2, lower, 1),
            (3, 2, upper, -1),
        )[way]
        return remote(
            self.gbuf.at[source, rows, :],
            self.gbuf.at[target, rows, :],
            self.sends.at[group, way],
            self.recvs.at[group, way],
            self.p.at_x(step),
        )

    def start(self, group):
        self.copy(group, 0).start()
        self.copy(group, 1).start()

    def forward(self, group):
        self.copy(group, 0).wait_recv()
        self.copy(group, 2).start()
        self.copy(group, 1).wait_recv()
        self.copy(group, 3).start()

    def landed(self, group):
        self.copy(group, 2).wait_recv()
        self.copy(group, 3).wait_recv()

    def finish(self, group):
        for way in range(4):
            self.copy(group, way).wait_send()


class Scatter:
    def __init__(self, place, terms, sbuf, rbuf, sends, recvs):
        self.p, self.terms, self.sbuf, self.rbuf, self.sends, self.recvs = place, terms, sbuf, rbuf, sends, recvs

    def rows(self, way, step):
        if step:
            return slice(0, WIDE)
        return slice(way * (WIDE // 2), (way + 1) * (WIDE // 2))

    def copy(self, group, way, step):
        rows = self.rows(way, step)
        return remote(
            self.sbuf.at[group, way, step, rows, :],
            self.rbuf.at[group, way, step, rows, :],
            self.sends.at[group, way, step],
            self.recvs.at[group, way, step],
            self.p.at_z(1 - 2 * way),
        )

    def step(self, group, step):
        for way in range(2):
            owner = lax.rem(self.p.z + (1 - 2 * way) * (NZ // 2 - step) + NZ, NZ)
            if step:
                self.copy(group, way, step - 1).wait_recv()
            for half in range(2):
                rows = slice(half * (WIDE // 2), (half + 1) * (WIDE // 2))
                if step == 0 and half != way:
                    continue
                total = self.terms[group, owner, rows, :]
                if step > 1 or (step == 1 and half == way):
                    total += self.rbuf[group, way, step - 1, rows, :].astype(jnp.float32)
                self.sbuf[group, way, step, rows, :] = total.astype(jnp.bfloat16)
            self.copy(group, way, step).start()

    def result(self, group):
        last = NZ // 2 - 1
        total = self.terms[group, self.p.z]
        for way in range(2):
            self.copy(group, way, last).wait_recv()
            total += self.rbuf[group, way, last].astype(jnp.float32)
        return total.T.astype(jnp.bfloat16)

    def finish(self, group):
        for way in range(2):
            for step in range(NZ // 2):
                self.copy(group, way, step).wait_send()


def weight_terms(group, abuf, gbuf, terms):
    rows = pl.ds(group * WIDE, WIDE)
    width = terms.shape[3]
    per = WIDE // width

    def columns(n, carry):
        cols = pl.ds(pl.multiple_of(n * WIDE, WIDE), WIDE)
        total = None
        for slot in range(NX):
            term = jnp.dot(gbuf[slot, rows, :], abuf[slot, :, cols], preferred_element_type=jnp.float32)
            total = term if total is None else total + term
        for k in range(per):
            terms[group, n * per + k] = total[:, k * width : (k + 1) * width]
        return carry

    lax.fori_loop(0, NZ // per, columns, 0)


class Span:
    def __init__(self, place, kbuf, vbuf, sends, recvs):
        self.p, self.bufs, self.sends, self.recvs = place, (kbuf, vbuf), sends, recvs

    def copy(self, which, hop):
        buf = self.bufs[which]
        source, target = (pl.ds(4, 2), pl.ds(2, 2)) if hop == 0 else (pl.ds(2, 2), pl.ds(0, 2))
        return remote(
            buf.at[source], buf.at[target], self.sends.at[which, hop], self.recvs.at[which, hop], self.p.at_c(1)
        )

    def finish(self):
        for which in range(2):
            for hop in range(2):
                self.copy(which, hop).wait_send()


class Return:
    def __init__(self, place, accs, sbuf, rbuf, sends, recvs):
        self.p, self.accs, self.sbuf, self.rbuf, self.sends, self.recvs = place, accs, sbuf, rbuf, sends, recvs

    def copy(self, which, hop):
        return remote(
            self.sbuf.at[which, hop],
            self.rbuf.at[which, hop],
            self.sends.at[which, hop],
            self.recvs.at[which, hop],
            self.p.at_c(-1),
        )

    def start(self, which, hop):
        if hop:
            self.copy(which, 0).wait_recv()
        for k in range(2):
            total = self.accs[which][2 * hop + k]
            if hop:
                total += self.rbuf[which, 0, k].astype(jnp.float32)
            self.sbuf[which, hop, k] = total.astype(jnp.bfloat16)
        self.copy(which, hop).start()

    def landed(self, which, factor, gbuf, row):
        self.copy(which, 1).wait_recv()
        for k in range(2):
            total = self.accs[which][4 + k] + self.rbuf[which, 1, k].astype(jnp.float32)
            gbuf[0, row : row + HEAD_SIZE, k * WIDE : (k + 1) * WIDE] = (total * factor).astype(jnp.bfloat16).T

    def finish(self):
        for which in range(2):
            for hop in range(2):
                self.copy(which, hop).wait_send()


def greet(place):
    barrier = pltpu.get_barrier_semaphore()
    others = [place.at_x(s) for s in (1, 2, 3)] + [place.at_y(s) for s in (1, 2, 3)]
    others += [place.sibling(), place.at_z(1), place.at_z(-1), place.at_c(1), place.at_c(-1)]
    for other in others:
        pl.semaphore_signal(barrier, inc=1, device_id=other, device_id_type=MESH)
    pl.semaphore_wait(barrier, len(others))


def doc_starts(docs, first, out):
    pos = first + lax.broadcasted_iota(jnp.int32, (1, out.shape[1]), 1)
    start = jnp.zeros_like(pos)
    end = jnp.int32(0)
    for n in range(docs.shape[0]):
        end = end + docs[n]
        start = jnp.where(pos >= end, end, start)
    out[...] = start


def attend(h, first, starts, kbuf, vbuf, kt, qh, gh, qt, gt, sc, dp, dk, dv, gbuf):
    f32, bf16 = jnp.float32, jnp.bfloat16
    scale = HEAD_SIZE**-0.5
    factor = scale * math.log2(math.e)
    near = lambda qs: slice(qs * WIDE, (qs + 1) * WIDE)
    row = lax.broadcasted_iota(jnp.int32, (WIDE, WIDE), 0)
    col = lax.broadcasted_iota(jnp.int32, (WIDE, WIDE), 1)
    base = first - 2 * qh.shape[1]
    tops, sums, deltas = [], [], []
    for qs in range(2):
        begin = starts[:, near(qs)] - base
        top = None
        for j in range(REACH):
            s = jnp.dot(kbuf[qs + j], qt[h, :, near(qs)], preferred_element_type=f32)
            seen = row >= begin - (qs + j) * WIDE
            if j == REACH - 1:
                seen &= row <= col
            s = jnp.where(seen, s, -jnp.inf)
            sc[qs, j] = s
            most = jnp.max(s, axis=0, keepdims=True)
            top = most if top is None else jnp.maximum(top, most)
        tops.append(top)
    for qs in range(2):
        shift = tops[qs] * factor
        total = mixed = None
        for j in range(REACH):
            p = jnp.exp2(sc[qs, j] * factor - shift)
            d = jnp.dot(vbuf[qs + j], gt[h, :, near(qs)], preferred_element_type=f32)
            sc[qs, j] = p
            dp[qs, j] = d
            a, b = jnp.sum(p, axis=0, keepdims=True), jnp.sum(p * d, axis=0, keepdims=True)
            total = a if total is None else total + a
            mixed = b if mixed is None else mixed + b
        inverse = 1.0 / total
        sums.append(inverse)
        deltas.append(mixed * inverse)
    for qs in range(2):
        dq = None
        for j in range(REACH):
            p = sc[qs, j] * sums[qs]
            ds = (p * (dp[qs, j] - deltas[qs])).astype(bf16)
            dv[qs + j] += jnp.dot(p.astype(bf16), gh[h, near(qs)], preferred_element_type=f32)
            dk[qs + j] += jnp.dot(ds, qh[h, near(qs)], preferred_element_type=f32)
            term = jnp.dot(kt[qs + j], ds, preferred_element_type=f32)
            dq = term if dq is None else dq + term
        gbuf[0, pl.ds(pl.multiple_of(h * HEAD_SIZE, HEAD_SIZE), HEAD_SIZE), near(qs)] = (dq * scale).astype(bf16)


def kernel(
    docs, act, q, k, v, g, wq, wk, wv,
    abuf, gbuf, terms, sbuf, rbuf, kbuf, vbuf, kt, qh, gh, qt, gt, sc, dp, dk, dv, starts, back_s, back_r,
    local, as_, ar_, gs_, gr_, ss_, sr_, ks_, kr_, bs_, br_,
):
    place = Place()
    acts = Acts(place, act, abuf, local, as_, ar_)
    gather = Gather(place, gbuf, gs_, gr_)
    scatter = Scatter(place, terms, sbuf, rbuf, ss_, sr_)
    span = Span(place, kbuf, vbuf, ks_, kr_)
    back = Return(place, (dk, dv), back_s, back_r, bs_, br_)
    heads = qh.shape[0]
    tokens = qh.shape[1]
    first = place.c * tokens
    for n in range(2):
        kbuf[4 + n] = k[n * WIDE : (n + 1) * WIDE, :]
        vbuf[4 + n] = v[n * WIDE : (n + 1) * WIDE, :]
    greet(place)
    span.copy(0, 0).start()
    span.copy(1, 0).start()
    acts.start()
    doc_starts(docs, first, starts)
    dk[...] = jnp.zeros_like(dk)
    dv[...] = jnp.zeros_like(dv)
    for h in range(heads):
        cols = slice(h * HEAD_SIZE, (h + 1) * HEAD_SIZE)
        qh[h] = q[:, cols]
        gh[h] = g[:, cols]
        qt[h] = q[:, cols].T
        gt[h] = g[:, cols].T
    for n in (4, 5):
        kt[n] = kbuf[n].T
    for which in range(2):
        span.copy(which, 0).wait_recv()
        span.copy(which, 1).start()
    for n in (2, 3):
        kt[n] = kbuf[n].T
    acts.spread_y()
    span.copy(0, 1).wait_recv()
    for n in (0, 1):
        kt[n] = kbuf[n].T
    span.copy(1, 1).wait_recv()

    def head(h, carry):
        attend(h, first, starts, kbuf, vbuf, kt, qh, gh, qt, gt, sc, dp, dk, dv, gbuf)
        gather.start(h)

        @pl.when(h == 0)
        def _():
            acts.spread_core()

        @pl.when(h > 0)
        def _():
            gather.forward(h - 1)

        return carry

    lax.fori_loop(0, heads, head, 0)
    back.start(0, 0)
    back.start(1, 0)
    gather.forward(3)
    acts.landed()
    gather.landed(0)
    gather.landed(1)
    weight_terms(0, abuf, gbuf, terms)
    scatter.step(0, 0)
    back.start(0, 1)
    back.start(1, 1)
    gather.landed(2)
    gather.landed(3)
    weight_terms(1, abuf, gbuf, terms)
    scatter.step(1, 0)
    scatter.step(0, 1)
    back.landed(0, HEAD_SIZE**-0.5, gbuf, 4 * HEAD_SIZE)
    gather.start(4)
    back.landed(1, 1.0, gbuf, 5 * HEAD_SIZE)
    gather.start(5)
    scatter.step(1, 1)
    scatter.step(0, 2)
    gather.forward(4)
    gather.forward(5)
    scatter.step(1, 2)
    scatter.step(0, 3)
    gather.landed(4)
    gather.landed(5)
    weight_terms(2, abuf, gbuf, terms)
    scatter.step(2, 0)
    scatter.step(1, 3)
    wq[:, 0:WIDE] = scatter.result(0)
    scatter.step(2, 1)
    wq[:, WIDE : 2 * WIDE] = scatter.result(1)
    scatter.step(2, 2)
    scatter.step(2, 3)
    both = scatter.result(2)
    wk[...] = both[:, 0:HEAD_SIZE]
    wv[...] = both[:, HEAD_SIZE:WIDE]
    acts.finish()
    span.finish()
    back.finish()
    for n in range(heads + 2):
        gather.finish(n)
    for group in range(GROUPS):
        scatter.finish(group)


def shards(doc_lengths, activations, queries, key_heads, head_values, output_gradient):
    tokens, features = activations.shape
    heads = queries.shape[1] // HEAD_SIZE
    quarter = features // NX
    chunk = quarter // NZ
    blocks = (SPAN + 1) * tokens // WIDE
    bf16, f32 = jnp.bfloat16, jnp.float32
    dma = pltpu.SemaphoreType.DMA
    vmem = pl.BlockSpec(memory_space=pltpu.VMEM)
    return pl.pallas_call(
        kernel,
        out_shape=(
            jax.ShapeDtypeStruct((chunk, heads * HEAD_SIZE), bf16),
            jax.ShapeDtypeStruct((chunk, HEAD_SIZE), bf16),
            jax.ShapeDtypeStruct((chunk, HEAD_SIZE), bf16),
        ),
        in_specs=[pl.BlockSpec(memory_space=pltpu.SMEM), pl.BlockSpec(memory_space=pl.ANY), vmem, vmem, vmem, vmem],
        out_specs=[vmem] * 3,
        scratch_shapes=[
            pltpu.VMEM((NX, tokens, quarter), bf16),
            pltpu.VMEM((NX, GROUPS * WIDE, tokens), bf16),
            pltpu.VMEM((GROUPS, NZ, WIDE, chunk), f32),
            pltpu.VMEM((GROUPS, 2, NZ // 2, WIDE, chunk), bf16),
            pltpu.VMEM((GROUPS, 2, NZ // 2, WIDE, chunk), bf16),
            pltpu.VMEM((blocks, WIDE, HEAD_SIZE), bf16),
            pltpu.VMEM((blocks, WIDE, HEAD_SIZE), bf16),
            pltpu.VMEM((blocks, HEAD_SIZE, WIDE), bf16),
            pltpu.VMEM((heads, tokens, HEAD_SIZE), bf16),
            pltpu.VMEM((heads, tokens, HEAD_SIZE), bf16),
            pltpu.VMEM((heads, HEAD_SIZE, tokens), bf16),
            pltpu.VMEM((heads, HEAD_SIZE, tokens), bf16),
            pltpu.VMEM((2, REACH, WIDE, WIDE), f32),
            pltpu.VMEM((2, REACH, WIDE, WIDE), f32),
            pltpu.VMEM((blocks, WIDE, HEAD_SIZE), f32),
            pltpu.VMEM((blocks, WIDE, HEAD_SIZE), f32),
            pltpu.VMEM((1, tokens), jnp.int32),
            pltpu.VMEM((2, 2, 2, WIDE, HEAD_SIZE), bf16),
            pltpu.VMEM((2, 2, 2, WIDE, HEAD_SIZE), bf16),
            dma,
            dma((10,)),
            dma((10,)),
            dma((heads + 2, 4)),
            dma((heads + 2, 4)),
            dma((GROUPS, 2, NZ // 2)),
            dma((GROUPS, 2, NZ // 2)),
            dma((2, 2)),
            dma((2, 2)),
            dma((2, 2)),
            dma((2, 2)),
        ],
        compiler_params=pltpu.CompilerParams(
            collective_id=0, has_side_effects=True, vmem_limit_bytes=48 * 2**20
        ),
    )(doc_lengths, activations, queries, key_heads, head_values, output_gradient)


def solution(mesh):
    return jax.shard_map(
        shards,
        mesh=mesh,
        in_specs=(
            P(),
            P("ctx", None),
            P("ctx", "tp"),
            P("ctx", "tp"),
            P("ctx", "tp"),
            P("ctx", "tp"),
        ),
        out_specs=(P("ctx", "tp"), P("ctx", "tp"), P("ctx", "tp")),
        check_vma=False,
    )
```

```python
import math

import jax
import jax.numpy as jnp
from jax import lax
from jax.experimental import pallas as pl
from jax.experimental.pallas import tpu as pltpu
from jax.sharding import PartitionSpec as P

HEAD_SIZE = 128
SPAN = 2
NX, NZ = 4, 8
NY, NCORE = 4, 2
WIDE = 256
REACH = 5
PARTS = ((0, 256), (256, 256), (512, 128), (640, 128))
MESH = pl.DeviceIdType.MESH


class Place:
    def __init__(self):
        self.c = lax.axis_index("ctx")
        self.t = lax.axis_index("tp")
        self.x = lax.div(self.c, NZ)
        self.z = lax.rem(self.c, NZ)
        self.y = lax.div(self.t, NCORE)
        self.core = lax.rem(self.t, NCORE)

    def at_x(self, step):
        return (lax.rem(self.x + step + NX, NX) * NZ + self.z, self.t)

    def at_z(self, step):
        return (self.x * NZ + lax.rem(self.z + step + NZ, NZ), self.t)

    def at_y(self, step):
        return (self.c, lax.rem(self.y + step + NY, NY) * NCORE + self.core)

    def at_c(self, step):
        count = NX * NZ
        return (lax.rem(self.c + step + count, count), self.t)

    def sibling(self):
        return (self.c, self.y * NCORE + 1 - self.core)

    def part(self, ystep, other_core):
        core = 1 - self.core if other_core else self.core
        return lax.rem(self.y + ystep + NY, NY) * NCORE + core


def remote(src, dst, send, recv, device):
    return pltpu.make_async_remote_copy(
        src_ref=src, dst_ref=dst, send_sem=send, recv_sem=recv, device_id=device, device_id_type=MESH
    )


class Acts:
    def __init__(self, place, act, abuf, local, sends, recvs):
        self.p, self.act, self.abuf, self.local, self.sends, self.recvs = place, act, abuf, local, sends, recvs
        self.tokens = act.shape[0]
        self.share = self.tokens // (NY * NCORE)
        self.quarter = act.shape[1] // NX

    def rows(self, part, begin=0, count=None):
        count = self.share if count is None else count
        return pl.ds(pl.multiple_of(part * self.share + begin, count), count)

    def own(self):
        cols = pl.ds(pl.multiple_of(self.p.x * self.quarter, self.quarter), self.quarter)
        return pltpu.make_async_copy(self.act.at[:, cols], self.abuf.at[0], self.local)

    def x_copy(self, step):
        there = lax.rem(self.p.x + step, NX)
        cols = pl.ds(pl.multiple_of(there * self.quarter, self.quarter), self.quarter)
        rows = self.rows(self.p.t)
        return remote(
            self.act.at[rows, cols],
            self.abuf.at[step, rows, :],
            self.sends.at[step - 1],
            self.recvs.at[step - 1],
            self.p.at_x(step),
        )

    def passed(self, rows, sem, device):
        piece = self.abuf.at[pl.ds(1, NX - 1), rows, :]
        return remote(piece, piece, self.sends.at[sem], self.recvs.at[sem], device)

    def y_copy(self, way, mine=True):
        step = 1 - 2 * way
        part = self.p.t if mine else self.p.part(-step, False)
        return self.passed(self.rows(part), 3 + way, self.p.at_y(step))

    def y_forward(self, way, mine=True):
        step = 1 - 2 * way
        half = self.share // 2
        rows = self.rows(self.p.part(-step if mine else 2, False), way * half, half)
        return self.passed(rows, 5 + way, self.p.at_y(step))

    def core_copy(self, which):
        return self.passed(self.rows(self.p.part((0, -1, 1, 2)[which], False)), 7 + which, self.p.sibling())

    def start(self):
        for step in (2, 1, 3):
            self.x_copy(step).start()
        self.own().start()

    def spread(self):
        for step in (1, 2, 3):
            self.x_copy(step).wait_recv()
        for way in range(2):
            self.y_copy(way).start()
        self.core_copy(0).start()

    def spread_on(self):
        for way in range(2):
            self.y_copy(way, False).wait_recv()
            self.y_forward(way).start()
        for way in range(2):
            self.core_copy(1 + way).start()

    def spread_last(self):
        for way in range(2):
            self.y_forward(way, False).wait_recv()
        self.core_copy(3).start()

    def landed(self):
        self.own().wait()
        for which in range(4):
            self.core_copy(which).wait_recv()

    def finish(self):
        for step in (1, 2, 3):
            self.x_copy(step).wait_send()
        for way in range(2):
            self.y_copy(way).wait_send()
            self.y_forward(way).wait_send()
        for which in range(4):
            self.core_copy(which).wait_send()


class Gather:
    def __init__(self, place, gbuf, sends, recvs):
        self.p, self.gbuf, self.sends, self.recvs = place, gbuf, sends, recvs
        self.tokens = gbuf.shape[1] // NX

    def copy(self, head, way):
        half = HEAD_SIZE // 2
        whole = pl.ds(pl.multiple_of(head * HEAD_SIZE, HEAD_SIZE), HEAD_SIZE)
        lower = pl.ds(pl.multiple_of(head * HEAD_SIZE, half), half)
        upper = pl.ds(pl.multiple_of(head * HEAD_SIZE + half, half), half)
        source, target, rows, step = ((0, 1, whole, 1), (0, 3, whole, -1), (1, 2, lower, 1), (3, 2, upper, -1))[way]
        return remote(
            self.gbuf.at[rows, pl.ds(source * self.tokens, self.tokens)],
            self.gbuf.at[rows, pl.ds(target * self.tokens, self.tokens)],
            self.sends.at[head, way],
            self.recvs.at[head, way],
            self.p.at_x(step),
        )

    def start(self, head):
        self.copy(head, 0).start()
        self.copy(head, 1).start()

    def forward(self, head):
        self.copy(head, 0).wait_recv()
        self.copy(head, 2).start()
        self.copy(head, 1).wait_recv()
        self.copy(head, 3).start()

    def landed(self, head):
        self.copy(head, 2).wait_recv()
        self.copy(head, 3).wait_recv()

    def finish(self, head):
        for way in range(4):
            self.copy(head, way).wait_send()


class Scatter:
    def __init__(self, place, terms, sbuf, rbuf, sends, recvs):
        self.p, self.terms, self.sbuf, self.rbuf, self.sends, self.recvs = place, terms, sbuf, rbuf, sends, recvs

    def rows(self, group, way, step):
        begin, count = PARTS[group]
        if step:
            return slice(begin, begin + count)
        return slice(begin + way * (count // 2), begin + (way + 1) * (count // 2))

    def copy(self, group, way, step):
        rows = self.rows(group, way, step)
        return remote(
            self.sbuf.at[way, step, rows, :],
            self.rbuf.at[way, step, rows, :],
            self.sends.at[group, way, step],
            self.recvs.at[group, way, step],
            self.p.at_z(1 - 2 * way),
        )

    def step(self, group, step):
        for way in range(2):
            owner = lax.rem(self.p.z + (1 - 2 * way) * (NZ // 2 - step) + NZ, NZ)
            if step:
                self.copy(group, way, step - 1).wait_recv()
            for half in range(2):
                if step == 0 and half != way:
                    continue
                rows = self.rows(group, half, 0)
                total = self.terms[owner, rows, :]
                if step > 1 or (step == 1 and half == way):
                    total += self.rbuf[way, step - 1, rows, :].astype(jnp.float32)
                self.sbuf[way, step, rows, :] = total.astype(jnp.bfloat16)
            self.copy(group, way, step).start()

    def result(self, group):
        last = NZ // 2 - 1
        rows = self.rows(group, 0, last)
        total = self.terms[self.p.z, rows, :]
        for way in range(2):
            self.copy(group, way, last).wait_recv()
            total += self.rbuf[way, last, rows, :].astype(jnp.float32)
        return total.T.astype(jnp.bfloat16)

    def finish(self, group):
        for way in range(2):
            for step in range(NZ // 2):
                self.copy(group, way, step).wait_send()


def weight_terms(group, abuf, gbuf, terms):
    begin, count = PARTS[group]
    rows = slice(begin, begin + count)
    width = terms.shape[2]
    per = WIDE // width

    def columns(n, carry):
        cols = pl.ds(pl.multiple_of(n * WIDE, WIDE), WIDE)
        acts = abuf[:, :, cols].reshape(gbuf.shape[1], WIDE)
        total = jnp.dot(gbuf[rows, :], acts, preferred_element_type=jnp.float32)
        for k in range(per):
            terms[n * per + k, rows, :] = total[:, k * width : (k + 1) * width]
        return carry

    lax.fori_loop(0, NZ // per, columns, 0)


class Span:
    def __init__(self, place, kbuf, vbuf, sends, recvs):
        self.p, self.bufs, self.sends, self.recvs = place, (kbuf, vbuf), sends, recvs

    def copy(self, which, hop):
        buf = self.bufs[which]
        source, target = (pl.ds(4, 2), pl.ds(2, 2)) if hop == 0 else (pl.ds(2, 2), pl.ds(0, 2))
        return remote(
            buf.at[source], buf.at[target], self.sends.at[which, hop], self.recvs.at[which, hop], self.p.at_c(1)
        )

    def finish(self):
        for which in range(2):
            for hop in range(2):
                self.copy(which, hop).wait_send()


class Return:
    def __init__(self, place, accs, sbuf, rbuf, sends, recvs):
        self.p, self.accs, self.sbuf, self.rbuf, self.sends, self.recvs = place, accs, sbuf, rbuf, sends, recvs

    def copy(self, which, hop):
        return remote(
            self.sbuf.at[which, hop],
            self.rbuf.at[which, hop],
            self.sends.at[which, hop],
            self.recvs.at[which, hop],
            self.p.at_c(-1),
        )

    def start(self, which, hop):
        if hop:
            self.copy(which, 0).wait_recv()
        for k in range(2):
            total = self.accs[which][2 * hop + k]
            if hop:
                total += self.rbuf[which, 0, k].astype(jnp.float32)
            self.sbuf[which, hop, k] = total.astype(jnp.bfloat16)
        self.copy(which, hop).start()

    def landed(self, which, factor, gbuf, row):
        self.copy(which, 1).wait_recv()
        for k in range(2):
            total = self.accs[which][4 + k] + self.rbuf[which, 1, k].astype(jnp.float32)
            gbuf[row : row + HEAD_SIZE, k * WIDE : (k + 1) * WIDE] = (total * factor).astype(jnp.bfloat16).T

    def finish(self):
        for which in range(2):
            for hop in range(2):
                self.copy(which, hop).wait_send()


def partners(place):
    others = [place.at_x(s) for s in (1, 2, 3)] + [place.at_y(s) for s in (1, -1)]
    return others + [place.sibling(), place.at_z(1), place.at_z(-1), place.at_c(1), place.at_c(-1)]


def doc_starts(docs, first, out):
    pos = first + lax.broadcasted_iota(jnp.int32, (1, out.shape[1]), 1)
    start = jnp.zeros_like(pos)
    end = jnp.int32(0)
    for n in range(docs.shape[0]):
        end = end + docs[n]
        start = jnp.where(pos >= end, end, start)
    out[...] = start


def near(qs):
    return slice(qs * WIDE, (qs + 1) * WIDE)


def reached(blocks):
    return [(qs, w, w - qs) for qs in range(2) for w in blocks if 0 <= w - qs < REACH]


def scores(h, blocks, base, starts, kbuf, qt, sc, top):
    row = lax.broadcasted_iota(jnp.int32, (WIDE, WIDE), 0)
    col = lax.broadcasted_iota(jnp.int32, (WIDE, WIDE), 1)
    tops = {}
    for qs, w, j in reached(blocks):
        s = jnp.dot(kbuf[w], qt[h, :, near(qs)], preferred_element_type=jnp.float32)
        seen = row >= starts[:, near(qs)] - (base + w * WIDE)
        if j == REACH - 1:
            seen &= row <= col
        s = jnp.where(seen, s, -jnp.inf)
        sc[h, qs, j] = s
        most = jnp.max(s, axis=0, keepdims=True)
        tops[qs] = jnp.maximum(tops[qs], most) if qs in tops else most
    for qs, most in tops.items():
        top[h, :, near(qs)] = jnp.maximum(top[h, :, near(qs)], most)


def value_products(h, blocks, vbuf, gt, dp):
    for qs, w, j in reached(blocks):
        dp[h, qs, j] = jnp.dot(vbuf[w], gt[h, :, near(qs)], preferred_element_type=jnp.float32)


def softmax(h, gh, sc, dp, top, inverse, mixed, dv):
    factor = HEAD_SIZE**-0.5 * math.log2(math.e)
    for qs in range(2):
        shift = top[h, :, near(qs)] * factor
        total = None
        for j in range(REACH):
            p = jnp.exp2(sc[h, qs, j] * factor - shift)
            sc[h, qs, j] = p
            part = jnp.sum(p, axis=0, keepdims=True)
            total = part if total is None else total + part
        inverse[h, :, near(qs)] = 1.0 / total
    for qs in range(2):
        scale = inverse[h, :, near(qs)]
        delta = None
        for j in range(REACH):
            p = sc[h, qs, j] * scale
            if qs + j >= 2:
                part = jnp.sum(p * dp[h, qs, j], axis=0, keepdims=True)
                delta = part if delta is None else delta + part
            dv[qs + j] += jnp.dot(p.astype(jnp.bfloat16), gh[h, near(qs)], preferred_element_type=jnp.float32)
        mixed[h, :, near(qs)] = delta


def score_grads(h, vbuf, kt, qh, gt, sc, dp, inverse, mixed, dk, gbuf):
    f32, bf16 = jnp.float32, jnp.bfloat16
    deltas = [mixed[h, :, near(qs)] for qs in range(2)]
    for qs, w, j in reached((0, 1)):
        d = jnp.dot(vbuf[w], gt[h, :, near(qs)], preferred_element_type=f32)
        dp[h, qs, j] = d
        deltas[qs] += jnp.sum(sc[h, qs, j] * inverse[h, :, near(qs)] * d, axis=0, keepdims=True)
    for qs in range(2):
        scale = inverse[h, :, near(qs)]
        dq = None
        for j in range(REACH):
            ds = (sc[h, qs, j] * scale * (dp[h, qs, j] - deltas[qs])).astype(bf16)
            dk[qs + j] += jnp.dot(ds, qh[h, near(qs)], preferred_element_type=f32)
            term = jnp.dot(kt[qs + j], ds, preferred_element_type=f32)
            dq = term if dq is None else dq + term
        rows = pl.ds(pl.multiple_of(h * HEAD_SIZE, HEAD_SIZE), HEAD_SIZE)
        gbuf[rows, near(qs)] = (dq * HEAD_SIZE**-0.5).astype(bf16)


def kernel(
    docs, act, q, k, v, g, wq, wk, wv,
    abuf, gbuf, terms, sbuf, rbuf, kbuf, vbuf, kt, qh, gh, qt, gt, sc, dp, dk, dv, starts, top, inverse, mixed,
    back_s, back_r, loads, local, as_, ar_, gs_, gr_, ss_, sr_, ks_, kr_, bs_, br_,
):
    place = Place()
    acts = Acts(place, act, abuf, local, as_, ar_)
    gather = Gather(place, gbuf, gs_, gr_)
    scatter = Scatter(place, terms, sbuf, rbuf, ss_, sr_)
    span = Span(place, kbuf, vbuf, ks_, kr_)
    back = Return(place, (dk, dv), back_s, back_r, bs_, br_)
    heads, tokens = qh.shape[0], qh.shape[1]
    first = place.c * tokens
    base = first - SPAN * tokens
    barrier = pltpu.get_barrier_semaphore()
    others = partners(place)
    for other in others:
        pl.semaphore_signal(barrier, inc=1, device_id=other, device_id_type=MESH)
    copies = [
        pltpu.make_async_copy(k, kbuf.at[pl.ds(4, 2)], loads.at[0]),
        pltpu.make_async_copy(v, vbuf.at[pl.ds(4, 2)], loads.at[1]),
    ]
    for h in range(heads):
        cols = pl.ds(h * HEAD_SIZE, HEAD_SIZE)
        copies.append(pltpu.make_async_copy(q.at[:, cols], qh.at[h], loads.at[2 + 2 * h]))
        copies.append(pltpu.make_async_copy(g.at[:, cols], gh.at[h], loads.at[3 + 2 * h]))
    for copy in copies:
        copy.start()
    doc_starts(docs, first, starts)
    dk[...] = jnp.zeros_like(dk)
    dv[...] = jnp.zeros_like(dv)
    top[...] = jnp.full_like(top, -jnp.inf)
    for copy in copies:
        copy.wait()
    pl.semaphore_wait(barrier, len(others))
    span.copy(0, 0).start()
    span.copy(1, 0).start()
    acts.start()

    def each_head(step):
        def body(h, carry):
            step(h)
            return carry

        lax.fori_loop(0, heads, body, 0)

    def turn(h):
        qt[h] = qh[h].T
        gt[h] = gh[h].T

    def own(h):
        scores(h, (4, 5), base, starts, kbuf, qt, sc, top)
        value_products(h, (4, 5), vbuf, gt, dp)

    def middle(h):
        scores(h, (2, 3), base, starts, kbuf, qt, sc, top)
        value_products(h, (2, 3), vbuf, gt, dp)

    def far(h):
        scores(h, (0, 1), base, starts, kbuf, qt, sc, top)
        softmax(h, gh, sc, dp, top, inverse, mixed, dv)

    def last(h):
        score_grads(h, vbuf, kt, qh, gt, sc, dp, inverse, mixed, dk, gbuf)
        gather.start(h)

        @pl.when(h == 2)
        def _():
            back.start(1, 1)
            acts.spread_on()

        @pl.when(h > 0)
        def _():
            gather.forward(h - 1)

    each_head(turn)
    span.copy(0, 0).wait_recv()
    span.copy(0, 1).start()
    each_head(own)
    span.copy(1, 0).wait_recv()
    span.copy(1, 1).start()
    each_head(middle)
    for n in (2, 3, 4, 5):
        kt[n] = kbuf[n].T
    span.copy(0, 1).wait_recv()
    for n in (0, 1):
        kt[n] = kbuf[n].T
    acts.spread()
    each_head(far)
    back.start(1, 0)
    span.copy(1, 1).wait_recv()
    each_head(last)
    back.start(0, 0)
    gather.forward(3)
    acts.spread_last()
    back.landed(1, 1.0, gbuf, 5 * HEAD_SIZE)
    gather.start(5)
    back.start(0, 1)
    acts.landed()
    gather.landed(0)
    gather.landed(1)
    weight_terms(0, abuf, gbuf, terms)
    scatter.step(0, 0)
    gather.forward(5)
    back.landed(0, HEAD_SIZE**-0.5, gbuf, 4 * HEAD_SIZE)
    gather.start(4)
    gather.landed(2)
    gather.landed(3)
    weight_terms(1, abuf, gbuf, terms)
    scatter.step(1, 0)
    scatter.step(0, 1)
    gather.landed(5)
    weight_terms(3, abuf, gbuf, terms)
    scatter.step(3, 0)
    gather.forward(4)
    scatter.step(0, 2)
    scatter.step(1, 1)
    scatter.step(3, 1)
    scatter.step(0, 3)
    scatter.step(1, 2)
    scatter.step(3, 2)
    gather.landed(4)
    weight_terms(2, abuf, gbuf, terms)
    scatter.step(2, 0)
    scatter.step(1, 3)
    scatter.step(3, 3)
    wq[:, 0:WIDE] = scatter.result(0)
    scatter.step(2, 1)
    wq[:, WIDE : 2 * WIDE] = scatter.result(1)
    scatter.step(2, 2)
    wv[...] = scatter.result(3)
    scatter.step(2, 3)
    wk[...] = scatter.result(2)
    acts.finish()
    span.finish()
    back.finish()
    for n in range(heads + 2):
        gather.finish(n)
    for group in range(len(PARTS)):
        scatter.finish(group)


def shards(doc_lengths, activations, queries, key_heads, head_values, output_gradient):
    tokens, features = activations.shape
    heads = queries.shape[1] // HEAD_SIZE
    quarter = features // NX
    chunk = quarter // NZ
    blocks = (SPAN + 1) * tokens // WIDE
    width = (heads + 2) * HEAD_SIZE
    bf16, f32 = jnp.bfloat16, jnp.float32
    dma = pltpu.SemaphoreType.DMA
    vmem = pl.BlockSpec(memory_space=pltpu.VMEM)
    return pl.pallas_call(
        kernel,
        out_shape=(
            jax.ShapeDtypeStruct((chunk, heads * HEAD_SIZE), bf16),
            jax.ShapeDtypeStruct((chunk, HEAD_SIZE), bf16),
            jax.ShapeDtypeStruct((chunk, HEAD_SIZE), bf16),
        ),
        in_specs=[pl.BlockSpec(memory_space=pltpu.SMEM)] + [pl.BlockSpec(memory_space=pl.ANY)] * 5,
        out_specs=[vmem] * 3,
        scratch_shapes=[
            pltpu.VMEM((NX, tokens, quarter), bf16),
            pltpu.VMEM((width, NX * tokens), bf16),
            pltpu.VMEM((NZ, width, chunk), f32),
            pltpu.VMEM((2, NZ // 2, width, chunk), bf16),
            pltpu.VMEM((2, NZ // 2, width, chunk), bf16),
            pltpu.VMEM((blocks, WIDE, HEAD_SIZE), bf16),
            pltpu.VMEM((blocks, WIDE, HEAD_SIZE), bf16),
            pltpu.VMEM((blocks, HEAD_SIZE, WIDE), bf16),
            pltpu.VMEM((heads, tokens, HEAD_SIZE), bf16),
            pltpu.VMEM((heads, tokens, HEAD_SIZE), bf16),
            pltpu.VMEM((heads, HEAD_SIZE, tokens), bf16),
            pltpu.VMEM((heads, HEAD_SIZE, tokens), bf16),
            pltpu.VMEM((heads, 2, REACH, WIDE, WIDE), f32),
            pltpu.VMEM((heads, 2, REACH, WIDE, WIDE), f32),
            pltpu.VMEM((blocks, WIDE, HEAD_SIZE), f32),
            pltpu.VMEM((blocks, WIDE, HEAD_SIZE), f32),
            pltpu.VMEM((1, tokens), jnp.int32),
            pltpu.VMEM((heads, 1, tokens), f32),
            pltpu.VMEM((heads, 1, tokens), f32),
            pltpu.VMEM((heads, 1, tokens), f32),
            pltpu.VMEM((2, 2, 2, WIDE, HEAD_SIZE), bf16),
            pltpu.VMEM((2, 2, 2, WIDE, HEAD_SIZE), bf16),
            dma((2 + 2 * heads,)),
            dma,
            dma((11,)),
            dma((11,)),
            dma((heads + 2, 4)),
            dma((heads + 2, 4)),
            dma((len(PARTS), 2, NZ // 2)),
            dma((len(PARTS), 2, NZ // 2)),
            dma((2, 2)),
            dma((2, 2)),
            dma((2, 2)),
            dma((2, 2)),
        ],
        compiler_params=pltpu.CompilerParams(
            collective_id=0, has_side_effects=True, vmem_limit_bytes=56 * 2**20
        ),
    )(
        doc_lengths,
        activations,
        queries,
        key_heads.reshape(-1, WIDE, HEAD_SIZE),
        head_values.reshape(-1, WIDE, HEAD_SIZE),
        output_gradient,
    )


def solution(mesh):
    return jax.shard_map(
        shards,
        mesh=mesh,
        in_specs=(
            P(),
            P("ctx", None),
            P("ctx", "tp"),
            P("ctx", "tp"),
            P("ctx", "tp"),
            P("ctx", "tp"),
        ),
        out_specs=(P("ctx", "tp"), P("ctx", "tp"), P("ctx", "tp")),
        check_vma=False,
    )
```

```python
import math

import jax
import jax.numpy as jnp
from jax import lax
from jax.experimental import pallas as pl
from jax.experimental.pallas import tpu as pltpu
from jax.sharding import PartitionSpec as P

HEAD_SIZE = 128
SPAN = 2
NX, NZ = 4, 8
NY, NCORE = 4, 2
WIDE = 256
REACH = 5
AHEAD = 96
PARTS = ((0, 256), (256, 256), (512, 128), (640, 128))
MESH = pl.DeviceIdType.MESH


class Place:
    def __init__(self):
        self.c = lax.axis_index("ctx")
        self.t = lax.axis_index("tp")
        self.x = lax.div(self.c, NZ)
        self.z = lax.rem(self.c, NZ)
        self.y = lax.div(self.t, NCORE)
        self.core = lax.rem(self.t, NCORE)

    def at_x(self, step):
        return (lax.rem(self.x + step + NX, NX) * NZ + self.z, self.t)

    def at_z(self, step):
        return (self.x * NZ + lax.rem(self.z + step + NZ, NZ), self.t)

    def at_y(self, step):
        return (self.c, lax.rem(self.y + step + NY, NY) * NCORE + self.core)

    def at_c(self, step):
        count = NX * NZ
        return (lax.rem(self.c + step + count, count), self.t)

    def sibling(self):
        return (self.c, self.y * NCORE + 1 - self.core)

    def part(self, ystep, other_core):
        core = 1 - self.core if other_core else self.core
        return lax.rem(self.y + ystep + NY, NY) * NCORE + core


def remote(src, dst, send, recv, device):
    return pltpu.make_async_remote_copy(
        src_ref=src, dst_ref=dst, send_sem=send, recv_sem=recv, device_id=device, device_id_type=MESH
    )


class Acts:
    def __init__(self, place, act, abuf, relay, local, sends, recvs):
        self.relay = relay
        self.p, self.act, self.abuf, self.local, self.sends, self.recvs = place, act, abuf, local, sends, recvs
        self.tokens = act.shape[0]
        self.share = self.tokens // (NY * NCORE)
        self.quarter = act.shape[1] // NX

    def rows(self, part, begin=0, count=None):
        count = self.share if count is None else count
        return pl.ds(pl.multiple_of(part * self.share + begin, count), count)

    def own(self):
        cols = pl.ds(pl.multiple_of(self.p.x * self.quarter, self.quarter), self.quarter)
        return pltpu.make_async_copy(self.act.at[:, cols], self.abuf.at[0], self.local)

    def quarter_of(self, step):
        there = lax.rem(self.p.x + step + NX, NX)
        return pl.ds(pl.multiple_of(there * self.quarter, self.quarter), self.quarter)

    def x_copy(self, way):
        step = 1 - 2 * way
        rows = self.rows(self.p.t)
        source, target = self.act.at[rows, self.quarter_of(step)], self.abuf.at[step % NX, rows, :]
        return remote(source, target, self.sends.at[way], self.recvs.at[way], self.p.at_x(step))

    def x_relay(self, way):
        half = self.share // 2
        source = self.act.at[self.rows(self.p.t, way * half, half), self.quarter_of(2)]
        device = self.p.at_x(1 - 2 * way)
        return remote(source, self.relay.at[way], self.sends.at[11 + way], self.recvs.at[11 + way], device)

    def x_forward(self, way):
        half = self.share // 2
        target = self.abuf.at[2, self.rows(self.p.t, way * half, half), :]
        device = self.p.at_x(1 - 2 * way)
        return remote(self.relay.at[way], target, self.sends.at[13 + way], self.recvs.at[13 + way], device)

    def passed(self, rows, sem, device):
        piece = self.abuf.at[pl.ds(1, NX - 1), rows, :]
        return remote(piece, piece, self.sends.at[sem], self.recvs.at[sem], device)

    def y_copy(self, way, mine=True):
        step = 1 - 2 * way
        part = self.p.t if mine else self.p.part(-step, False)
        return self.passed(self.rows(part), 3 + way, self.p.at_y(step))

    def y_forward(self, way, mine=True):
        step = 1 - 2 * way
        half = self.share // 2
        rows = self.rows(self.p.part(-step if mine else 2, False), way * half, half)
        return self.passed(rows, 5 + way, self.p.at_y(step))

    def core_copy(self, which):
        return self.passed(self.rows(self.p.part((0, -1, 1, 2)[which], False)), 7 + which, self.p.sibling())

    def start(self):
        for way in range(2):
            self.x_relay(way).start()
        for way in range(2):
            self.x_copy(way).start()

    def forward(self):
        for way in range(2):
            self.x_relay(way).wait_recv()
            self.x_forward(way).start()

    def spread(self):
        for way in range(2):
            self.x_copy(way).wait_recv()
            self.x_forward(way).wait_recv()
        for way in range(2):
            self.y_copy(way).start()
        self.core_copy(0).start()

    def spread_on(self):
        for way in range(2):
            self.y_copy(way, False).wait_recv()
            self.y_forward(way).start()
        for way in range(2):
            self.core_copy(1 + way).start()

    def spread_last(self):
        for way in range(2):
            self.y_forward(way, False).wait_recv()
        self.core_copy(3).start()

    def landed(self):
        self.own().wait()
        for which in range(4):
            self.core_copy(which).wait_recv()

    def finish(self):
        for way in range(2):
            self.x_copy(way).wait_send()
            self.x_relay(way).wait_send()
            self.x_forward(way).wait_send()
            self.y_copy(way).wait_send()
            self.y_forward(way).wait_send()
        for which in range(4):
            self.core_copy(which).wait_send()


class Gather:
    def __init__(self, place, gbuf, sends, recvs):
        self.p, self.gbuf, self.sends, self.recvs = place, gbuf, sends, recvs
        self.tokens = gbuf.shape[1] // NX

    def copy(self, head, way):
        rest = HEAD_SIZE - AHEAD
        whole = pl.ds(pl.multiple_of(head * HEAD_SIZE, HEAD_SIZE), HEAD_SIZE)
        lower = pl.ds(pl.multiple_of(head * HEAD_SIZE, HEAD_SIZE), AHEAD)
        upper = pl.ds(pl.multiple_of(head * HEAD_SIZE + AHEAD, rest), rest)
        source, target, rows, step = ((0, 1, whole, 1), (0, 3, whole, -1), (1, 2, lower, 1), (3, 2, upper, -1))[way]
        return remote(
            self.gbuf.at[rows, pl.ds(source * self.tokens, self.tokens)],
            self.gbuf.at[rows, pl.ds(target * self.tokens, self.tokens)],
            self.sends.at[head, way],
            self.recvs.at[head, way],
            self.p.at_x(step),
        )

    def start(self, head):
        self.copy(head, 0).start()
        self.copy(head, 1).start()

    def forward(self, head):
        self.copy(head, 0).wait_recv()
        self.copy(head, 2).start()
        self.copy(head, 1).wait_recv()
        self.copy(head, 3).start()

    def landed(self, head):
        self.copy(head, 2).wait_recv()
        self.copy(head, 3).wait_recv()

    def finish(self, head):
        for way in range(4):
            self.copy(head, way).wait_send()


class Scatter:
    def __init__(self, place, terms, sbuf, rbuf, sends, recvs):
        self.p, self.terms, self.sbuf, self.rbuf, self.sends, self.recvs = place, terms, sbuf, rbuf, sends, recvs

    def rows(self, group, way, step):
        begin, count = PARTS[group]
        if step:
            return slice(begin, begin + count)
        return slice(begin + way * (count // 2), begin + (way + 1) * (count // 2))

    def copy(self, group, way, step):
        rows = self.rows(group, way, step)
        return remote(
            self.sbuf.at[way, step, rows, :],
            self.rbuf.at[way, step, rows, :],
            self.sends.at[group, way, step],
            self.recvs.at[group, way, step],
            self.p.at_z(1 - 2 * way),
        )

    def step(self, group, step):
        for way in range(2):
            owner = lax.rem(self.p.z + (1 - 2 * way) * (NZ // 2 - step) + NZ, NZ)
            if step:
                self.copy(group, way, step - 1).wait_recv()
            for half in range(2):
                if step == 0 and half != way:
                    continue
                rows = self.rows(group, half, 0)
                total = self.terms[owner, rows, :]
                if step > 1 or (step == 1 and half == way):
                    total += self.rbuf[way, step - 1, rows, :].astype(jnp.float32)
                self.sbuf[way, step, rows, :] = total.astype(jnp.bfloat16)
            self.copy(group, way, step).start()

    def result(self, group):
        last = NZ // 2 - 1
        rows = self.rows(group, 0, last)
        total = self.terms[self.p.z, rows, :]
        for way in range(2):
            self.copy(group, way, last).wait_recv()
            total += self.rbuf[way, last, rows, :].astype(jnp.float32)
        return total.astype(jnp.bfloat16)

    def finish(self, group):
        for way in range(2):
            for step in range(NZ // 2):
                self.copy(group, way, step).wait_send()


class Direct:
    def __init__(self, place, group, terms, sbuf, rbuf, sends, recvs):
        self.p, self.terms, self.sbuf, self.rbuf, self.sends, self.recvs = place, terms, sbuf, rbuf, sends, recvs
        begin, count = PARTS[group]
        self.rows = slice(begin, begin + count)

    def copy(self, step):
        n = step - 1
        return remote(self.sbuf.at[n], self.rbuf.at[n], self.sends.at[n], self.recvs.at[n], self.p.at_z(step))

    def start(self):
        for step in (4, 3, 5, 2, 6, 1, 7):
            owner = lax.rem(self.p.z + step, NZ)
            self.sbuf[step - 1] = self.terms[owner, self.rows, :].astype(jnp.bfloat16)
            self.copy(step).start()

    def result(self):
        total = self.terms[self.p.z, self.rows, :]
        for step in (1, 7, 2, 6, 3, 5, 4):
            self.copy(step).wait_recv()
            total += self.rbuf[step - 1].astype(jnp.float32)
        return total.astype(jnp.bfloat16)

    def finish(self):
        for step in range(1, NZ):
            self.copy(step).wait_send()


def weight_terms(group, abuf, gbuf, terms):
    begin, count = PARTS[group]
    rows = slice(begin, begin + count)
    width = terms.shape[2]
    per = WIDE // width

    def columns(n, carry):
        cols = pl.ds(pl.multiple_of(n * WIDE, WIDE), WIDE)
        acts = abuf[:, :, cols].reshape(gbuf.shape[1], WIDE)
        total = jnp.dot(gbuf[rows, :], acts, preferred_element_type=jnp.float32)
        for k in range(per):
            terms[n * per + k, rows, :] = total[:, k * width : (k + 1) * width]
        return carry

    lax.fori_loop(0, NZ // per, columns, 0)


class Span:
    def __init__(self, place, kbuf, vbuf, sends, recvs):
        self.p, self.bufs, self.sends, self.recvs = place, (kbuf, vbuf), sends, recvs

    def copy(self, which, hop):
        buf = self.bufs[which]
        source, target = (pl.ds(4, 2), pl.ds(2, 2)) if hop == 0 else (pl.ds(2, 2), pl.ds(0, 2))
        return remote(
            buf.at[source], buf.at[target], self.sends.at[which, hop], self.recvs.at[which, hop], self.p.at_c(1)
        )

    def finish(self):
        for which in range(2):
            for hop in range(2):
                self.copy(which, hop).wait_send()


class Return:
    def __init__(self, place, accs, sbuf, rbuf, sends, recvs):
        self.p, self.accs, self.sbuf, self.rbuf, self.sends, self.recvs = place, accs, sbuf, rbuf, sends, recvs

    def copy(self, which, hop):
        return remote(
            self.sbuf.at[which, hop],
            self.rbuf.at[which, hop],
            self.sends.at[which, hop],
            self.recvs.at[which, hop],
            self.p.at_c(-1),
        )

    def start(self, which, hop):
        if hop:
            self.copy(which, 0).wait_recv()
        for k in range(2):
            total = self.accs[which][2 * hop + k]
            if hop:
                total += self.rbuf[which, 0, k].astype(jnp.float32)
            self.sbuf[which, hop, k] = total.astype(jnp.bfloat16)
        self.copy(which, hop).start()

    def landed(self, which, factor, gbuf, row):
        self.copy(which, 1).wait_recv()
        for k in range(2):
            total = self.accs[which][4 + k] + self.rbuf[which, 1, k].astype(jnp.float32)
            gbuf[row : row + HEAD_SIZE, k * WIDE : (k + 1) * WIDE] = (total * factor).astype(jnp.bfloat16).T

    def finish(self):
        for which in range(2):
            for hop in range(2):
                self.copy(which, hop).wait_send()


def partners(place):
    others = [place.at_x(s) for s in (1, -1)] + [place.at_y(s) for s in (1, -1)]
    return others + [place.sibling(), place.at_c(1), place.at_c(-1)] + [place.at_z(s) for s in range(1, NZ)]


def doc_starts(docs, first, out):
    pos = first + lax.broadcasted_iota(jnp.int32, (1, out.shape[1]), 1)
    start = jnp.zeros_like(pos)
    end = jnp.int32(0)
    for n in range(docs.shape[0]):
        end = end + docs[n]
        start = jnp.where(pos >= end, end, start)
    out[...] = start


def near(qs):
    return slice(qs * WIDE, (qs + 1) * WIDE)


def reached(blocks):
    return [(qs, w, w - qs) for qs in range(2) for w in blocks if 0 <= w - qs < REACH]


def scores(h, blocks, base, starts, kbuf, qt, sc, top):
    row = lax.broadcasted_iota(jnp.int32, (WIDE, WIDE), 0)
    col = lax.broadcasted_iota(jnp.int32, (WIDE, WIDE), 1)
    tops = {}
    for qs, w, j in reached(blocks):
        s = jnp.dot(kbuf[w], qt[h, :, near(qs)], preferred_element_type=jnp.float32)
        seen = row >= starts[:, near(qs)] - (base + w * WIDE)
        if j == REACH - 1:
            seen &= row <= col
        s = jnp.where(seen, s, -jnp.inf)
        sc[h, qs, j] = s
        most = jnp.max(s, axis=0, keepdims=True)
        tops[qs] = jnp.maximum(tops[qs], most) if qs in tops else most
    for qs, most in tops.items():
        top[h, :, near(qs)] = jnp.maximum(top[h, :, near(qs)], most)


def value_products(h, blocks, vbuf, gt, dp):
    for qs, w, j in reached(blocks):
        dp[h, qs, j] = jnp.dot(vbuf[w], gt[h, :, near(qs)], preferred_element_type=jnp.float32)


def softmax(h, gh, sc, dp, top, inverse, mixed, dv):
    factor = HEAD_SIZE**-0.5 * math.log2(math.e)
    for qs in range(2):
        shift = top[h, :, near(qs)] * factor
        total = None
        for j in range(REACH):
            p = jnp.exp2(sc[h, qs, j] * factor - shift)
            sc[h, qs, j] = p
            part = jnp.sum(p, axis=0, keepdims=True)
            total = part if total is None else total + part
        inverse[h, :, near(qs)] = 1.0 / total
    for qs in range(2):
        scale = inverse[h, :, near(qs)]
        delta = None
        for j in range(REACH):
            p = sc[h, qs, j] * scale
            if qs + j >= 2:
                part = jnp.sum(p * dp[h, qs, j], axis=0, keepdims=True)
                delta = part if delta is None else delta + part
            dv[qs + j] += jnp.dot(p.astype(jnp.bfloat16), gh[h, near(qs)], preferred_element_type=jnp.float32)
        mixed[h, :, near(qs)] = delta


def score_grads(h, vbuf, kt, qh, gt, sc, dp, inverse, mixed, dk, gbuf):
    f32, bf16 = jnp.float32, jnp.bfloat16
    deltas = [mixed[h, :, near(qs)] for qs in range(2)]
    for qs, w, j in reached((0, 1)):
        d = jnp.dot(vbuf[w], gt[h, :, near(qs)], preferred_element_type=f32)
        dp[h, qs, j] = d
        deltas[qs] += jnp.sum(sc[h, qs, j] * inverse[h, :, near(qs)] * d, axis=0, keepdims=True)
    for qs in range(2):
        scale = inverse[h, :, near(qs)]
        dq = None
        for j in range(REACH):
            ds = (sc[h, qs, j] * scale * (dp[h, qs, j] - deltas[qs])).astype(bf16)
            dk[qs + j] += jnp.dot(ds, qh[h, near(qs)], preferred_element_type=f32)
            term = jnp.dot(kt[qs + j], ds, preferred_element_type=f32)
            dq = term if dq is None else dq + term
        rows = pl.ds(pl.multiple_of(h * HEAD_SIZE, HEAD_SIZE), HEAD_SIZE)
        gbuf[rows, near(qs)] = (dq * HEAD_SIZE**-0.5).astype(bf16)


def kernel(
    docs, act, q, k, v, g, out,
    abuf, relay, gbuf, terms, sbuf, rbuf, kbuf, vbuf, kt, qh, gh, qt, gt, sc, dp, dk, dv, starts, top, inverse, mixed,
    back_s, back_r, dir_s, dir_r, loads, local, as_, ar_, gs_, gr_, ss_, sr_, ks_, kr_, bs_, br_, ds_, dr_,
):
    place = Place()
    acts = Acts(place, act, abuf, relay, local, as_, ar_)
    gather = Gather(place, gbuf, gs_, gr_)
    scatter = Scatter(place, terms, sbuf, rbuf, ss_, sr_)
    span = Span(place, kbuf, vbuf, ks_, kr_)
    back = Return(place, (dk, dv), back_s, back_r, bs_, br_)
    direct = Direct(place, 2, terms, dir_s, dir_r, ds_, dr_)
    heads, tokens = qh.shape[0], qh.shape[1]
    first = place.c * tokens
    base = first - SPAN * tokens
    barrier = pltpu.get_barrier_semaphore()
    others = partners(place)
    for other in others:
        pl.semaphore_signal(barrier, inc=1, device_id=other, device_id_type=MESH)
    copies = [
        pltpu.make_async_copy(k, kbuf.at[pl.ds(4, 2)], loads.at[0]),
        pltpu.make_async_copy(v, vbuf.at[pl.ds(4, 2)], loads.at[1]),
    ]
    for h in range(heads):
        cols = pl.ds(h * HEAD_SIZE, HEAD_SIZE)
        copies.append(pltpu.make_async_copy(q.at[:, cols], qh.at[h], loads.at[2 + 2 * h]))
        copies.append(pltpu.make_async_copy(g.at[:, cols], gh.at[h], loads.at[3 + 2 * h]))
    for copy in copies:
        copy.start()
    for copy in copies[:2]:
        copy.wait()
    pl.semaphore_wait(barrier, len(others))
    span.copy(0, 0).start()
    span.copy(1, 0).start()
    acts.own().start()
    doc_starts(docs, first, starts)
    dk[...] = jnp.zeros_like(dk)
    dv[...] = jnp.zeros_like(dv)
    top[...] = jnp.full_like(top, -jnp.inf)
    for copy in copies[2:]:
        copy.wait()

    def each_head(step):
        def body(h, carry):
            step(h)
            return carry

        lax.fori_loop(0, heads, body, 0)

    def turn(h):
        qt[h] = qh[h].T
        gt[h] = gh[h].T

    def own(h):
        scores(h, (4, 5), base, starts, kbuf, qt, sc, top)
        value_products(h, (4, 5), vbuf, gt, dp)

    def middle(h):
        scores(h, (2, 3), base, starts, kbuf, qt, sc, top)
        value_products(h, (2, 3), vbuf, gt, dp)

    def far(h):
        scores(h, (0, 1), base, starts, kbuf, qt, sc, top)
        softmax(h, gh, sc, dp, top, inverse, mixed, dv)

    def last(h):
        score_grads(h, vbuf, kt, qh, gt, sc, dp, inverse, mixed, dk, gbuf)
        gather.start(h)

        @pl.when(h == 1)
        def _():
            back.start(1, 1)

        @pl.when(h == 2)
        def _():
            acts.spread()

    each_head(turn)
    span.copy(0, 0).wait_recv()
    span.copy(0, 1).start()
    each_head(own)
    span.copy(1, 0).wait_recv()
    span.copy(1, 1).start()
    acts.start()
    each_head(middle)
    for n in (2, 3, 4, 5):
        kt[n] = kbuf[n].T
    span.copy(0, 1).wait_recv()
    for n in (0, 1):
        kt[n] = kbuf[n].T
    each_head(far)
    back.start(1, 0)
    acts.forward()
    span.copy(1, 1).wait_recv()
    each_head(last)
    back.start(0, 0)
    gather.forward(0)
    back.landed(1, 1.0, gbuf, 5 * HEAD_SIZE)
    gather.start(5)
    gather.forward(1)
    back.start(0, 1)
    gather.forward(2)
    acts.spread_on()
    gather.forward(3)
    back.landed(0, HEAD_SIZE**-0.5, gbuf, 4 * HEAD_SIZE)
    gather.start(4)
    acts.spread_last()
    gather.forward(5)
    gather.landed(0)
    gather.landed(1)
    acts.landed()
    weight_terms(0, abuf, gbuf, terms)
    scatter.step(0, 0)
    gather.landed(2)
    gather.landed(3)
    weight_terms(1, abuf, gbuf, terms)
    scatter.step(1, 0)
    gather.forward(4)
    scatter.step(0, 1)
    gather.landed(5)
    weight_terms(3, abuf, gbuf, terms)
    scatter.step(3, 0)
    scatter.step(1, 1)
    scatter.step(0, 2)
    gather.landed(4)
    weight_terms(2, abuf, gbuf, terms)
    direct.start()
    scatter.step(3, 1)
    scatter.step(1, 2)
    scatter.step(0, 3)
    scatter.step(3, 2)
    scatter.step(1, 3)
    out[0:WIDE, :] = scatter.result(0)
    scatter.step(3, 3)
    out[WIDE : 2 * WIDE, :] = scatter.result(1)
    out[4 * HEAD_SIZE : 5 * HEAD_SIZE, :] = direct.result()
    out[5 * HEAD_SIZE : 6 * HEAD_SIZE, :] = scatter.result(3)
    acts.finish()
    span.finish()
    back.finish()
    direct.finish()
    for n in range(heads + 2):
        gather.finish(n)
    for group in (0, 1, 3):
        scatter.finish(group)


def turned(total, wq, wk, wv):
    columns = wq.shape[1]
    for n in range(columns // HEAD_SIZE):
        rows = slice(n * HEAD_SIZE, (n + 1) * HEAD_SIZE)
        wq[:, rows] = total[rows, :].T
    wk[...] = total[columns : columns + HEAD_SIZE, :].T
    wv[...] = total[columns + HEAD_SIZE : columns + 2 * HEAD_SIZE, :].T


def shards(doc_lengths, activations, queries, key_heads, head_values, output_gradient):
    tokens, features = activations.shape
    heads = queries.shape[1] // HEAD_SIZE
    quarter = features // NX
    chunk = quarter // NZ
    blocks = (SPAN + 1) * tokens // WIDE
    width = (heads + 2) * HEAD_SIZE
    bf16, f32 = jnp.bfloat16, jnp.float32
    dma = pltpu.SemaphoreType.DMA
    vmem = pl.BlockSpec(memory_space=pltpu.VMEM)
    total = pl.pallas_call(
        kernel,
        out_shape=jax.ShapeDtypeStruct((width, chunk), bf16),
        in_specs=[pl.BlockSpec(memory_space=pltpu.SMEM)] + [pl.BlockSpec(memory_space=pl.ANY)] * 5,
        out_specs=vmem,
        scratch_shapes=[
            pltpu.VMEM((NX, tokens, quarter), bf16),
            pltpu.VMEM((2, tokens // (2 * NY * NCORE), quarter), bf16),
            pltpu.VMEM((width, NX * tokens), bf16),
            pltpu.VMEM((NZ, width, chunk), f32),
            pltpu.VMEM((2, NZ // 2, width, chunk), bf16),
            pltpu.VMEM((2, NZ // 2, width, chunk), bf16),
            pltpu.VMEM((blocks, WIDE, HEAD_SIZE), bf16),
            pltpu.VMEM((blocks, WIDE, HEAD_SIZE), bf16),
            pltpu.VMEM((blocks, HEAD_SIZE, WIDE), bf16),
            pltpu.VMEM((heads, tokens, HEAD_SIZE), bf16),
            pltpu.VMEM((heads, tokens, HEAD_SIZE), bf16),
            pltpu.VMEM((heads, HEAD_SIZE, tokens), bf16),
            pltpu.VMEM((heads, HEAD_SIZE, tokens), bf16),
            pltpu.VMEM((heads, 2, REACH, WIDE, WIDE), f32),
            pltpu.VMEM((heads, 2, REACH, WIDE, WIDE), f32),
            pltpu.VMEM((blocks, WIDE, HEAD_SIZE), f32),
            pltpu.VMEM((blocks, WIDE, HEAD_SIZE), f32),
            pltpu.VMEM((1, tokens), jnp.int32),
            pltpu.VMEM((heads, 1, tokens), f32),
            pltpu.VMEM((heads, 1, tokens), f32),
            pltpu.VMEM((heads, 1, tokens), f32),
            pltpu.VMEM((2, 2, 2, WIDE, HEAD_SIZE), bf16),
            pltpu.VMEM((2, 2, 2, WIDE, HEAD_SIZE), bf16),
            pltpu.VMEM((NZ - 1, HEAD_SIZE, chunk), bf16),
            pltpu.VMEM((NZ - 1, HEAD_SIZE, chunk), bf16),
            dma((2 + 2 * heads,)),
            dma,
            dma((15,)),
            dma((15,)),
            dma((heads + 2, 4)),
            dma((heads + 2, 4)),
            dma((len(PARTS), 2, NZ // 2)),
            dma((len(PARTS), 2, NZ // 2)),
            dma((2, 2)),
            dma((2, 2)),
            dma((2, 2)),
            dma((2, 2)),
            dma((NZ - 1,)),
            dma((NZ - 1,)),
        ],
        compiler_params=pltpu.CompilerParams(
            collective_id=0, has_side_effects=True, vmem_limit_bytes=56 * 2**20
        ),
    )(
        doc_lengths,
        activations,
        queries,
        key_heads.reshape(-1, WIDE, HEAD_SIZE),
        head_values.reshape(-1, WIDE, HEAD_SIZE),
        output_gradient,
    )
    return pl.pallas_call(
        turned,
        out_shape=(
            jax.ShapeDtypeStruct((chunk, heads * HEAD_SIZE), bf16),
            jax.ShapeDtypeStruct((chunk, HEAD_SIZE), bf16),
            jax.ShapeDtypeStruct((chunk, HEAD_SIZE), bf16),
        ),
        in_specs=[vmem],
        out_specs=[vmem] * 3,
    )(total)


def solution(mesh):
    return jax.shard_map(
        shards,
        mesh=mesh,
        in_specs=(
            P(),
            P("ctx", None),
            P("ctx", "tp"),
            P("ctx", "tp"),
            P("ctx", "tp"),
            P("ctx", "tp"),
        ),
        out_specs=(P("ctx", "tp"), P("ctx", "tp"), P("ctx", "tp")),
        check_vma=False,
    )
```

```python
import math

import jax
import jax.numpy as jnp
from jax import lax
from jax.experimental import pallas as pl
from jax.experimental.pallas import tpu as pltpu
from jax.sharding import PartitionSpec as P

HEAD_SIZE = 128
SPAN = 2
NX, NZ = 4, 8
NY, NCORE = 4, 2
WIDE = 256
REACH = 5
AHEAD = 96
PARTS = ((0, 256), (256, 256), (512, 256))
MESH = pl.DeviceIdType.MESH


class Place:
    def __init__(self):
        self.c = lax.axis_index("ctx")
        self.t = lax.axis_index("tp")
        self.x = lax.div(self.c, NZ)
        self.z = lax.rem(self.c, NZ)
        self.y = lax.div(self.t, NCORE)
        self.core = lax.rem(self.t, NCORE)

    def at_x(self, step):
        return (lax.rem(self.x + step + NX, NX) * NZ + self.z, self.t)

    def at_z(self, step):
        return (self.x * NZ + lax.rem(self.z + step + NZ, NZ), self.t)

    def at_y(self, step):
        return (self.c, lax.rem(self.y + step + NY, NY) * NCORE + self.core)

    def at_c(self, step):
        count = NX * NZ
        return (lax.rem(self.c + step + count, count), self.t)

    def sibling(self):
        return (self.c, self.y * NCORE + 1 - self.core)

    def part(self, ystep, other_core):
        core = 1 - self.core if other_core else self.core
        return lax.rem(self.y + ystep + NY, NY) * NCORE + core


def remote(src, dst, send, recv, device):
    return pltpu.make_async_remote_copy(
        src_ref=src, dst_ref=dst, send_sem=send, recv_sem=recv, device_id=device, device_id_type=MESH
    )


class Acts:
    def __init__(self, place, act, abuf, relay, local, sends, recvs):
        self.relay = relay
        self.p, self.act, self.abuf, self.local, self.sends, self.recvs = place, act, abuf, local, sends, recvs
        self.tokens = act.shape[0]
        self.share = self.tokens // (NY * NCORE)
        self.quarter = act.shape[1] // NX

    def rows(self, part, begin=0, count=None):
        count = self.share if count is None else count
        return pl.ds(pl.multiple_of(part * self.share + begin, count), count)

    def own(self):
        cols = pl.ds(pl.multiple_of(self.p.x * self.quarter, self.quarter), self.quarter)
        return pltpu.make_async_copy(self.act.at[:, cols], self.abuf.at[0], self.local)

    def quarter_of(self, step):
        there = lax.rem(self.p.x + step + NX, NX)
        return pl.ds(pl.multiple_of(there * self.quarter, self.quarter), self.quarter)

    def x_copy(self, way):
        step = 1 - 2 * way
        rows = self.rows(self.p.t)
        source, target = self.act.at[rows, self.quarter_of(step)], self.abuf.at[step % NX, rows, :]
        return remote(source, target, self.sends.at[way], self.recvs.at[way], self.p.at_x(step))

    def x_relay(self, way):
        half = self.share // 2
        source = self.act.at[self.rows(self.p.t, way * half, half), self.quarter_of(2)]
        device = self.p.at_x(1 - 2 * way)
        return remote(source, self.relay.at[way], self.sends.at[2 + way], self.recvs.at[2 + way], device)

    def x_forward(self, way):
        half = self.share // 2
        target = self.abuf.at[2, self.rows(self.p.t, way * half, half), :]
        device = self.p.at_x(1 - 2 * way)
        return remote(self.relay.at[way], target, self.sends.at[4 + way], self.recvs.at[4 + way], device)

    def passed(self, slot, rows, sem, device):
        piece = self.abuf.at[slot, rows, :]
        return remote(piece, piece, self.sends.at[sem], self.recvs.at[sem], device)

    def y_copy(self, slot, way, mine=True):
        step = 1 - 2 * way
        part = self.p.t if mine else self.p.part(-step, False)
        return self.passed(slot, self.rows(part), 8 * slot + way, self.p.at_y(step))

    def y_forward(self, slot, way, mine=True):
        step = 1 - 2 * way
        half = self.share // 2
        rows = self.rows(self.p.part(-step if mine else 2, False), way * half, half)
        return self.passed(slot, rows, 8 * slot + 2 + way, self.p.at_y(step))

    def core_copy(self, slot, which):
        rows = self.rows(self.p.part((0, -1, 1, 2)[which], False))
        return self.passed(slot, rows, 8 * slot + 4 + which, self.p.sibling())

    def start(self):
        for way in range(2):
            self.x_relay(way).start()
        for way in range(2):
            self.x_copy(way).start()

    def forward(self):
        for way in range(2):
            self.x_relay(way).wait_recv()
            self.x_forward(way).start()

    def spread(self, slot):
        if slot == 2:
            for way in range(2):
                self.x_forward(way).wait_recv()
        else:
            self.x_copy(slot // 2).wait_recv()
        for way in range(2):
            self.y_copy(slot, way).start()
        self.core_copy(slot, 0).start()

    def spread_on(self, slot):
        for way in range(2):
            self.y_copy(slot, way, False).wait_recv()
            self.y_forward(slot, way).start()
        for way in range(2):
            self.core_copy(slot, 1 + way).start()

    def spread_last(self, slot):
        for way in range(2):
            self.y_forward(slot, way, False).wait_recv()
        self.core_copy(slot, 3).start()

    def landed(self):
        self.own().wait()
        for slot in range(1, NX):
            for which in range(4):
                self.core_copy(slot, which).wait_recv()

    def finish(self):
        for way in range(2):
            self.x_copy(way).wait_send()
            self.x_relay(way).wait_send()
            self.x_forward(way).wait_send()
        for slot in range(1, NX):
            for way in range(2):
                self.y_copy(slot, way).wait_send()
                self.y_forward(slot, way).wait_send()
            for which in range(4):
                self.core_copy(slot, which).wait_send()


class Gather:
    def __init__(self, place, gbuf, sends, recvs):
        self.p, self.gbuf, self.sends, self.recvs = place, gbuf, sends, recvs
        self.tokens = gbuf.shape[1] // NX

    def copy(self, head, way):
        rest = HEAD_SIZE - AHEAD
        whole = pl.ds(pl.multiple_of(head * HEAD_SIZE, HEAD_SIZE), HEAD_SIZE)
        lower = pl.ds(pl.multiple_of(head * HEAD_SIZE, HEAD_SIZE), AHEAD)
        upper = pl.ds(pl.multiple_of(head * HEAD_SIZE + AHEAD, rest), rest)
        source, target, rows, step = ((0, 1, whole, 1), (0, 3, whole, -1), (1, 2, lower, 1), (3, 2, upper, -1))[way]
        return remote(
            self.gbuf.at[rows, pl.ds(source * self.tokens, self.tokens)],
            self.gbuf.at[rows, pl.ds(target * self.tokens, self.tokens)],
            self.sends.at[head, way],
            self.recvs.at[head, way],
            self.p.at_x(step),
        )

    def start(self, head):
        self.copy(head, 0).start()
        self.copy(head, 1).start()

    def forward(self, head):
        self.copy(head, 0).wait_recv()
        self.copy(head, 2).start()
        self.copy(head, 1).wait_recv()
        self.copy(head, 3).start()

    def landed(self, head):
        self.copy(head, 2).wait_recv()
        self.copy(head, 3).wait_recv()

    def finish(self, head):
        for way in range(4):
            self.copy(head, way).wait_send()


class Scatter:
    def __init__(self, place, terms, sbuf, rbuf, sends, recvs):
        self.p, self.terms, self.sbuf, self.rbuf, self.sends, self.recvs = place, terms, sbuf, rbuf, sends, recvs

    def rows(self, group, way, step):
        begin, count = PARTS[group]
        if step:
            return slice(begin, begin + count)
        return slice(begin + way * (count // 2), begin + (way + 1) * (count // 2))

    def copy(self, group, way, step):
        rows = self.rows(group, way, step)
        return remote(
            self.sbuf.at[way, step, rows, :],
            self.rbuf.at[way, step, rows, :],
            self.sends.at[group, way, step],
            self.recvs.at[group, way, step],
            self.p.at_z(1 - 2 * way),
        )

    def step(self, group, step):
        for way in range(2):
            owner = lax.rem(self.p.z + (1 - 2 * way) * (NZ // 2 - step) + NZ, NZ)
            if step:
                self.copy(group, way, step - 1).wait_recv()
            for half in range(2):
                if step == 0 and half != way:
                    continue
                rows = self.rows(group, half, 0)
                total = self.terms[owner, rows, :]
                if step > 1 or (step == 1 and half == way):
                    total += self.rbuf[way, step - 1, rows, :].astype(jnp.float32)
                self.sbuf[way, step, rows, :] = total.astype(jnp.bfloat16)
            self.copy(group, way, step).start()

    def result(self, group):
        last = NZ // 2 - 1
        rows = self.rows(group, 0, last)
        total = self.terms[self.p.z, rows, :]
        for way in range(2):
            self.copy(group, way, last).wait_recv()
            total += self.rbuf[way, last, rows, :].astype(jnp.float32)
        return total.astype(jnp.bfloat16)

    def finish(self, group):
        for way in range(2):
            for step in range(NZ // 2):
                self.copy(group, way, step).wait_send()


def weight_terms(group, abuf, gbuf, terms):
    begin, count = PARTS[group]
    rows = slice(begin, begin + count)
    width = terms.shape[2]
    per = WIDE // width

    def columns(n, carry):
        cols = pl.ds(pl.multiple_of(n * WIDE, WIDE), WIDE)
        acts = abuf[:, :, cols].reshape(gbuf.shape[1], WIDE)
        total = jnp.dot(gbuf[rows, :], acts, preferred_element_type=jnp.float32)
        for k in range(per):
            terms[n * per + k, rows, :] = total[:, k * width : (k + 1) * width]
        return carry

    lax.fori_loop(0, NZ // per, columns, 0)


class Span:
    def __init__(self, place, kbuf, vbuf, sends, recvs):
        self.p, self.bufs, self.sends, self.recvs = place, (kbuf, vbuf), sends, recvs

    def copy(self, which, hop):
        buf = self.bufs[which]
        source, target = (pl.ds(4, 2), pl.ds(2, 2)) if hop == 0 else (pl.ds(2, 2), pl.ds(0, 2))
        return remote(
            buf.at[source], buf.at[target], self.sends.at[which, hop], self.recvs.at[which, hop], self.p.at_c(1)
        )

    def finish(self):
        for which in range(2):
            for hop in range(2):
                self.copy(which, hop).wait_send()


class Return:
    def __init__(self, place, accs, sbuf, rbuf, sends, recvs):
        self.p, self.accs, self.sbuf, self.rbuf, self.sends, self.recvs = place, accs, sbuf, rbuf, sends, recvs

    def copy(self, which, hop):
        return remote(
            self.sbuf.at[which, hop],
            self.rbuf.at[which, hop],
            self.sends.at[which, hop],
            self.recvs.at[which, hop],
            self.p.at_c(-1),
        )

    def start(self, which, hop):
        if hop:
            self.copy(which, 0).wait_recv()
        for k in range(2):
            total = self.accs[which][2 * hop + k]
            if hop:
                total += self.rbuf[which, 0, k].astype(jnp.float32)
            self.sbuf[which, hop, k] = total.astype(jnp.bfloat16)
        self.copy(which, hop).start()

    def landed(self, which, factor, gbuf, row):
        self.copy(which, 1).wait_recv()
        for k in range(2):
            total = self.accs[which][4 + k] + self.rbuf[which, 1, k].astype(jnp.float32)
            gbuf[row : row + HEAD_SIZE, k * WIDE : (k + 1) * WIDE] = (total * factor).astype(jnp.bfloat16).T

    def finish(self):
        for which in range(2):
            for hop in range(2):
                self.copy(which, hop).wait_send()


def partners(place):
    others = [place.at_x(s) for s in (1, -1)] + [place.at_y(s) for s in (1, -1)]
    return others + [place.sibling(), place.at_c(1), place.at_c(-1)] + [place.at_z(1), place.at_z(-1)]


def doc_starts(docs, first, out):
    pos = first + lax.broadcasted_iota(jnp.int32, (1, out.shape[1]), 1)
    start = jnp.zeros_like(pos)
    end = jnp.int32(0)
    for n in range(docs.shape[0]):
        end = end + docs[n]
        start = jnp.where(pos >= end, end, start)
    out[...] = start


def near(qs):
    return slice(qs * WIDE, (qs + 1) * WIDE)


def reached(blocks):
    return [(qs, w, w - qs) for qs in range(2) for w in blocks if 0 <= w - qs < REACH]


def scores(h, blocks, base, starts, kbuf, qt, sc, top):
    row = lax.broadcasted_iota(jnp.int32, (WIDE, WIDE), 0)
    col = lax.broadcasted_iota(jnp.int32, (WIDE, WIDE), 1)
    tops = {}
    for qs, w, j in reached(blocks):
        s = jnp.dot(kbuf[w], qt[h, :, near(qs)], preferred_element_type=jnp.float32)
        seen = row >= starts[:, near(qs)] - (base + w * WIDE)
        if j == REACH - 1:
            seen &= row <= col
        s = jnp.where(seen, s, -jnp.inf)
        sc[h, qs, j] = s
        most = jnp.max(s, axis=0, keepdims=True)
        tops[qs] = jnp.maximum(tops[qs], most) if qs in tops else most
    for qs, most in tops.items():
        top[h, :, near(qs)] = jnp.maximum(top[h, :, near(qs)], most)


def value_products(h, blocks, vbuf, gt, dp):
    for qs, w, j in reached(blocks):
        dp[h, qs, j] = jnp.dot(vbuf[w], gt[h, :, near(qs)], preferred_element_type=jnp.float32)


def softmax(h, gh, sc, dp, top, inverse, mixed, dv):
    factor = HEAD_SIZE**-0.5 * math.log2(math.e)
    for qs in range(2):
        shift = top[h, :, near(qs)] * factor
        total = None
        for j in range(REACH):
            p = jnp.exp2(sc[h, qs, j] * factor - shift)
            sc[h, qs, j] = p
            part = jnp.sum(p, axis=0, keepdims=True)
            total = part if total is None else total + part
        inverse[h, :, near(qs)] = 1.0 / total
    for qs in range(2):
        scale = inverse[h, :, near(qs)]
        delta = None
        for j in range(REACH):
            p = sc[h, qs, j] * scale
            if qs + j >= 2:
                part = jnp.sum(p * dp[h, qs, j], axis=0, keepdims=True)
                delta = part if delta is None else delta + part
            dv[qs + j] += jnp.dot(p.astype(jnp.bfloat16), gh[h, near(qs)], preferred_element_type=jnp.float32)
        mixed[h, :, near(qs)] = delta


def score_grads(h, vbuf, kt, qh, gt, sc, dp, inverse, mixed, dk, gbuf):
    f32, bf16 = jnp.float32, jnp.bfloat16
    deltas = [mixed[h, :, near(qs)] for qs in range(2)]
    for qs, w, j in reached((0, 1)):
        d = jnp.dot(vbuf[w], gt[h, :, near(qs)], preferred_element_type=f32)
        dp[h, qs, j] = d
        deltas[qs] += jnp.sum(sc[h, qs, j] * inverse[h, :, near(qs)] * d, axis=0, keepdims=True)
    for qs in range(2):
        scale = inverse[h, :, near(qs)]
        dq = None
        for j in range(REACH):
            ds = (sc[h, qs, j] * scale * (dp[h, qs, j] - deltas[qs])).astype(bf16)
            dk[qs + j] += jnp.dot(ds, qh[h, near(qs)], preferred_element_type=f32)
            term = jnp.dot(kt[qs + j], ds, preferred_element_type=f32)
            dq = term if dq is None else dq + term
        rows = pl.ds(pl.multiple_of(h * HEAD_SIZE, HEAD_SIZE), HEAD_SIZE)
        gbuf[rows, near(qs)] = (dq * HEAD_SIZE**-0.5).astype(bf16)


def kernel(
    docs, act, q, k, v, g, out,
    abuf, relay, gbuf, terms, sbuf, rbuf, kbuf, vbuf, kt, qh, gh, qt, gt, sc, dp, dk, dv, starts, top, inverse, mixed,
    back_s, back_r, loads, local, as_, ar_, gs_, gr_, ss_, sr_, ks_, kr_, bs_, br_,
):
    place = Place()
    acts = Acts(place, act, abuf, relay, local, as_, ar_)
    gather = Gather(place, gbuf, gs_, gr_)
    scatter = Scatter(place, terms, sbuf, rbuf, ss_, sr_)
    span = Span(place, kbuf, vbuf, ks_, kr_)
    back = Return(place, (dk, dv), back_s, back_r, bs_, br_)
    heads, tokens = qh.shape[0], qh.shape[1]
    first = place.c * tokens
    base = first - SPAN * tokens
    barrier = pltpu.get_barrier_semaphore()
    others = partners(place)
    for other in others:
        pl.semaphore_signal(barrier, inc=1, device_id=other, device_id_type=MESH)
    copies = [
        pltpu.make_async_copy(k, kbuf.at[pl.ds(4, 2)], loads.at[0]),
        pltpu.make_async_copy(v, vbuf.at[pl.ds(4, 2)], loads.at[1]),
    ]
    for h in range(heads):
        cols = pl.ds(h * HEAD_SIZE, HEAD_SIZE)
        copies.append(pltpu.make_async_copy(q.at[:, cols], qh.at[h], loads.at[2 + 2 * h]))
        copies.append(pltpu.make_async_copy(g.at[:, cols], gh.at[h], loads.at[3 + 2 * h]))
    for copy in copies:
        copy.start()
    for copy in copies[:2]:
        copy.wait()
    pl.semaphore_wait(barrier, len(others))
    span.copy(0, 0).start()
    span.copy(1, 0).start()
    acts.own().start()
    doc_starts(docs, first, starts)
    dk[...] = jnp.zeros_like(dk)
    dv[...] = jnp.zeros_like(dv)
    top[...] = jnp.full_like(top, -jnp.inf)
    for copy in copies[2:]:
        copy.wait()

    def each_head(step):
        def body(h, carry):
            step(h)
            return carry

        lax.fori_loop(0, heads, body, 0)

    def turn(h):
        qt[h] = qh[h].T
        gt[h] = gh[h].T

    def own(h):
        scores(h, (4, 5), base, starts, kbuf, qt, sc, top)
        value_products(h, (4, 5), vbuf, gt, dp)

    def middle(h):
        scores(h, (2, 3), base, starts, kbuf, qt, sc, top)
        value_products(h, (2, 3), vbuf, gt, dp)

    def far(h):
        scores(h, (0, 1), base, starts, kbuf, qt, sc, top)
        softmax(h, gh, sc, dp, top, inverse, mixed, dv)

    def last(h):
        score_grads(h, vbuf, kt, qh, gt, sc, dp, inverse, mixed, dk, gbuf)

        @pl.when(h < 2)
        def _():
            gather.start(h)

    each_head(turn)
    span.copy(0, 0).wait_recv()
    span.copy(0, 1).start()
    acts.start()
    each_head(own)
    span.copy(1, 0).wait_recv()
    span.copy(1, 1).start()
    each_head(middle)
    for n in (2, 3, 4, 5):
        kt[n] = kbuf[n].T
    span.copy(0, 1).wait_recv()
    for n in (0, 1):
        kt[n] = kbuf[n].T
    each_head(far)
    back.start(1, 0)
    acts.forward()
    acts.spread(1)
    acts.spread(3)
    span.copy(1, 1).wait_recv()
    each_head(last)
    back.start(0, 0)
    back.start(1, 1)
    gather.start(2)
    gather.start(3)
    acts.spread(2)
    gather.forward(0)
    back.landed(1, 1.0, gbuf, 5 * HEAD_SIZE)
    gather.start(5)
    acts.spread_on(1)
    acts.spread_on(3)
    gather.forward(1)
    back.start(0, 1)
    gather.forward(2)
    acts.spread_on(2)
    acts.spread_last(1)
    acts.spread_last(3)
    gather.forward(3)
    back.landed(0, HEAD_SIZE**-0.5, gbuf, 4 * HEAD_SIZE)
    gather.start(4)
    acts.spread_last(2)
    gather.forward(5)
    gather.landed(0)
    gather.landed(1)
    acts.landed()
    weight_terms(0, abuf, gbuf, terms)
    scatter.step(0, 0)
    gather.forward(4)
    gather.landed(2)
    gather.landed(3)
    weight_terms(1, abuf, gbuf, terms)
    scatter.step(1, 0)
    scatter.step(0, 1)
    gather.landed(5)
    gather.landed(4)
    weight_terms(2, abuf, gbuf, terms)
    scatter.step(2, 0)
    scatter.step(1, 1)
    scatter.step(0, 2)
    scatter.step(2, 1)
    scatter.step(1, 2)
    scatter.step(0, 3)
    scatter.step(2, 2)
    scatter.step(1, 3)
    out[0:WIDE, :] = scatter.result(0)
    scatter.step(2, 3)
    out[WIDE : 2 * WIDE, :] = scatter.result(1)
    out[2 * WIDE : 3 * WIDE, :] = scatter.result(2)
    acts.finish()
    span.finish()
    back.finish()
    for n in range(heads + 2):
        gather.finish(n)
    for group in range(len(PARTS)):
        scatter.finish(group)


def turned(total, wq, wk, wv):
    columns = wq.shape[1]
    for n in range(columns // HEAD_SIZE):
        rows = slice(n * HEAD_SIZE, (n + 1) * HEAD_SIZE)
        wq[:, rows] = total[rows, :].T
    wk[...] = total[columns : columns + HEAD_SIZE, :].T
    wv[...] = total[columns + HEAD_SIZE : columns + 2 * HEAD_SIZE, :].T


def shards(doc_lengths, activations, queries, key_heads, head_values, output_gradient):
    tokens, features = activations.shape
    heads = queries.shape[1] // HEAD_SIZE
    quarter = features // NX
    chunk = quarter // NZ
    blocks = (SPAN + 1) * tokens // WIDE
    width = (heads + 2) * HEAD_SIZE
    bf16, f32 = jnp.bfloat16, jnp.float32
    dma = pltpu.SemaphoreType.DMA
    vmem = pl.BlockSpec(memory_space=pltpu.VMEM)
    total = pl.pallas_call(
        kernel,
        out_shape=jax.ShapeDtypeStruct((width, chunk), bf16),
        in_specs=[pl.BlockSpec(memory_space=pltpu.SMEM)] + [pl.BlockSpec(memory_space=pl.ANY)] * 5,
        out_specs=vmem,
        scratch_shapes=[
            pltpu.VMEM((NX, tokens, quarter), bf16),
            pltpu.VMEM((2, tokens // (2 * NY * NCORE), quarter), bf16),
            pltpu.VMEM((width, NX * tokens), bf16),
            pltpu.VMEM((NZ, width, chunk), f32),
            pltpu.VMEM((2, NZ // 2, width, chunk), bf16),
            pltpu.VMEM((2, NZ // 2, width, chunk), bf16),
            pltpu.VMEM((blocks, WIDE, HEAD_SIZE), bf16),
            pltpu.VMEM((blocks, WIDE, HEAD_SIZE), bf16),
            pltpu.VMEM((blocks, HEAD_SIZE, WIDE), bf16),
            pltpu.VMEM((heads, tokens, HEAD_SIZE), bf16),
            pltpu.VMEM((heads, tokens, HEAD_SIZE), bf16),
            pltpu.VMEM((heads, HEAD_SIZE, tokens), bf16),
            pltpu.VMEM((heads, HEAD_SIZE, tokens), bf16),
            pltpu.VMEM((heads, 2, REACH, WIDE, WIDE), f32),
            pltpu.VMEM((heads, 2, REACH, WIDE, WIDE), f32),
            pltpu.VMEM((blocks, WIDE, HEAD_SIZE), f32),
            pltpu.VMEM((blocks, WIDE, HEAD_SIZE), f32),
            pltpu.VMEM((1, tokens), jnp.int32),
            pltpu.VMEM((heads, 1, tokens), f32),
            pltpu.VMEM((heads, 1, tokens), f32),
            pltpu.VMEM((heads, 1, tokens), f32),
            pltpu.VMEM((2, 2, 2, WIDE, HEAD_SIZE), bf16),
            pltpu.VMEM((2, 2, 2, WIDE, HEAD_SIZE), bf16),
            dma((2 + 2 * heads,)),
            dma,
            dma((8 * NX,)),
            dma((8 * NX,)),
            dma((heads + 2, 4)),
            dma((heads + 2, 4)),
            dma((len(PARTS), 2, NZ // 2)),
            dma((len(PARTS), 2, NZ // 2)),
            dma((2, 2)),
            dma((2, 2)),
            dma((2, 2)),
            dma((2, 2)),
        ],
        compiler_params=pltpu.CompilerParams(
            collective_id=0, has_side_effects=True, vmem_limit_bytes=56 * 2**20
        ),
    )(
        doc_lengths,
        activations,
        queries,
        key_heads.reshape(-1, WIDE, HEAD_SIZE),
        head_values.reshape(-1, WIDE, HEAD_SIZE),
        output_gradient,
    )
    return pl.pallas_call(
        turned,
        out_shape=(
            jax.ShapeDtypeStruct((chunk, heads * HEAD_SIZE), bf16),
            jax.ShapeDtypeStruct((chunk, HEAD_SIZE), bf16),
            jax.ShapeDtypeStruct((chunk, HEAD_SIZE), bf16),
        ),
        in_specs=[vmem],
        out_specs=[vmem] * 3,
    )(total)


def solution(mesh):
    return jax.shard_map(
        shards,
        mesh=mesh,
        in_specs=(
            P(),
            P("ctx", None),
            P("ctx", "tp"),
            P("ctx", "tp"),
            P("ctx", "tp"),
            P("ctx", "tp"),
        ),
        out_specs=(P("ctx", "tp"), P("ctx", "tp"), P("ctx", "tp")),
        check_vma=False,
    )
```

```python
import math

import jax
import jax.numpy as jnp
from jax import lax
from jax.experimental import pallas as pl
from jax.experimental.pallas import tpu as pltpu
from jax.sharding import PartitionSpec as P

HEAD_SIZE = 128
SPAN = 2
NX, NZ = 4, 8
NY, NCORE = 4, 2
WIDE = 256
REACH = 5
AHEAD = 96
PARTS = ((0, 256), (256, 256), (512, 256))
MESH = pl.DeviceIdType.MESH


class Place:
    def __init__(self):
        self.c = lax.axis_index("ctx")
        self.t = lax.axis_index("tp")
        self.x = lax.div(self.c, NZ)
        self.z = lax.rem(self.c, NZ)
        self.y = lax.div(self.t, NCORE)
        self.core = lax.rem(self.t, NCORE)

    def at_x(self, step):
        return (lax.rem(self.x + step + NX, NX) * NZ + self.z, self.t)

    def at_z(self, step):
        return (self.x * NZ + lax.rem(self.z + step + NZ, NZ), self.t)

    def at_y(self, step):
        return (self.c, lax.rem(self.y + step + NY, NY) * NCORE + self.core)

    def at_c(self, step):
        count = NX * NZ
        return (lax.rem(self.c + step + count, count), self.t)

    def sibling(self):
        return (self.c, self.y * NCORE + 1 - self.core)

    def part(self, ystep, other_core):
        core = 1 - self.core if other_core else self.core
        return lax.rem(self.y + ystep + NY, NY) * NCORE + core


def remote(src, dst, send, recv, device):
    return pltpu.make_async_remote_copy(
        src_ref=src, dst_ref=dst, send_sem=send, recv_sem=recv, device_id=device, device_id_type=MESH
    )


class Acts:
    def __init__(self, place, act, abuf, relay, local, sends, recvs):
        self.relay = relay
        self.p, self.act, self.abuf, self.local, self.sends, self.recvs = place, act, abuf, local, sends, recvs
        self.tokens = act.shape[0]
        self.share = self.tokens // (NY * NCORE)
        self.quarter = act.shape[1] // NX

    def rows(self, part, begin=0, count=None):
        count = self.share if count is None else count
        return pl.ds(pl.multiple_of(part * self.share + begin, count), count)

    def own(self):
        cols = pl.ds(pl.multiple_of(self.p.x * self.quarter, self.quarter), self.quarter)
        return pltpu.make_async_copy(self.act.at[:, cols], self.abuf.at[0], self.local)

    def quarter_of(self, step):
        there = lax.rem(self.p.x + step + NX, NX)
        return pl.ds(pl.multiple_of(there * self.quarter, self.quarter), self.quarter)

    def x_copy(self, way):
        step = 1 - 2 * way
        rows = self.rows(self.p.t)
        source, target = self.act.at[rows, self.quarter_of(step)], self.abuf.at[step % NX, rows, :]
        return remote(source, target, self.sends.at[way], self.recvs.at[way], self.p.at_x(step))

    def x_relay(self, way):
        half = self.share // 2
        source = self.act.at[self.rows(self.p.t, way * half, half), self.quarter_of(2)]
        device = self.p.at_x(1 - 2 * way)
        return remote(source, self.relay.at[way], self.sends.at[2 + way], self.recvs.at[2 + way], device)

    def x_forward(self, way):
        half = self.share // 2
        target = self.abuf.at[2, self.rows(self.p.t, way * half, half), :]
        device = self.p.at_x(1 - 2 * way)
        return remote(self.relay.at[way], target, self.sends.at[4 + way], self.recvs.at[4 + way], device)

    def passed(self, slot, rows, sem, device):
        piece = self.abuf.at[slot, rows, :]
        return remote(piece, piece, self.sends.at[sem], self.recvs.at[sem], device)

    def y_copy(self, slot, way, mine=True):
        step = 1 - 2 * way
        part = self.p.t if mine else self.p.part(-step, False)
        return self.passed(slot, self.rows(part), 8 * slot + way, self.p.at_y(step))

    def y_forward(self, slot, way, mine=True):
        step = 1 - 2 * way
        half = self.share // 2
        rows = self.rows(self.p.part(-step if mine else 2, False), way * half, half)
        return self.passed(slot, rows, 8 * slot + 2 + way, self.p.at_y(step))

    def core_copy(self, slot, which):
        rows = self.rows(self.p.part((0, -1, 1, 2)[which], False))
        return self.passed(slot, rows, 8 * slot + 4 + which, self.p.sibling())

    def start(self):
        for way in range(2):
            self.x_relay(way).start()
        for way in range(2):
            self.x_copy(way).start()

    def forward(self):
        for way in range(2):
            self.x_relay(way).wait_recv()
            self.x_forward(way).start()

    def spread(self, slot):
        if slot == 2:
            for way in range(2):
                self.x_forward(way).wait_recv()
        else:
            self.x_copy(slot // 2).wait_recv()
        for way in range(2):
            self.y_copy(slot, way).start()
        self.core_copy(slot, 0).start()

    def spread_on(self, slot):
        for way in range(2):
            self.y_copy(slot, way, False).wait_recv()
            self.y_forward(slot, way).start()
        for way in range(2):
            self.core_copy(slot, 1 + way).start()

    def spread_last(self, slot):
        for way in range(2):
            self.y_forward(slot, way, False).wait_recv()
        self.core_copy(slot, 3).start()

    def landed(self):
        self.own().wait()
        for slot in range(1, NX):
            for which in range(4):
                self.core_copy(slot, which).wait_recv()

    def finish(self):
        for way in range(2):
            self.x_copy(way).wait_send()
            self.x_relay(way).wait_send()
            self.x_forward(way).wait_send()
        for slot in range(1, NX):
            for way in range(2):
                self.y_copy(slot, way).wait_send()
                self.y_forward(slot, way).wait_send()
            for which in range(4):
                self.core_copy(slot, which).wait_send()


class Gather:
    def __init__(self, place, gbuf, sends, recvs):
        self.p, self.gbuf, self.sends, self.recvs = place, gbuf, sends, recvs
        self.tokens = gbuf.shape[1] // NX

    def copy(self, head, way):
        rest = HEAD_SIZE - AHEAD
        whole = pl.ds(pl.multiple_of(head * HEAD_SIZE, HEAD_SIZE), HEAD_SIZE)
        lower = pl.ds(pl.multiple_of(head * HEAD_SIZE, HEAD_SIZE), AHEAD)
        upper = pl.ds(pl.multiple_of(head * HEAD_SIZE + AHEAD, rest), rest)
        source, target, rows, step = ((0, 1, whole, 1), (0, 3, whole, -1), (1, 2, lower, 1), (3, 2, upper, -1))[way]
        return remote(
            self.gbuf.at[rows, pl.ds(source * self.tokens, self.tokens)],
            self.gbuf.at[rows, pl.ds(target * self.tokens, self.tokens)],
            self.sends.at[head, way],
            self.recvs.at[head, way],
            self.p.at_x(step),
        )

    def start(self, head):
        self.copy(head, 0).start()
        self.copy(head, 1).start()

    def forward(self, head):
        self.copy(head, 0).wait_recv()
        self.copy(head, 2).start()
        self.copy(head, 1).wait_recv()
        self.copy(head, 3).start()

    def landed(self, head):
        self.copy(head, 2).wait_recv()
        self.copy(head, 3).wait_recv()

    def finish(self, head):
        for way in range(4):
            self.copy(head, way).wait_send()


class Scatter:
    def __init__(self, place, terms, sbuf, rbuf, sends, recvs):
        self.p, self.terms, self.sbuf, self.rbuf, self.sends, self.recvs = place, terms, sbuf, rbuf, sends, recvs

    def rows(self, group, way, step):
        begin, count = PARTS[group]
        if step:
            return slice(begin, begin + count)
        return slice(begin + way * (count // 2), begin + (way + 1) * (count // 2))

    def copy(self, group, way, step):
        rows = self.rows(group, way, step)
        return remote(
            self.sbuf.at[way, step, rows, :],
            self.rbuf.at[way, step, rows, :],
            self.sends.at[group, way, step],
            self.recvs.at[group, way, step],
            self.p.at_z(1 - 2 * way),
        )

    def step(self, group, step):
        for way in range(2):
            owner = lax.rem(self.p.z + (1 - 2 * way) * (NZ // 2 - step) + NZ, NZ)
            if step:
                self.copy(group, way, step - 1).wait_recv()
            for half in range(2):
                if step == 0 and half != way:
                    continue
                rows = self.rows(group, half, 0)
                total = self.terms[owner, rows, :]
                if step > 1 or (step == 1 and half == way):
                    total += self.rbuf[way, step - 1, rows, :].astype(jnp.float32)
                self.sbuf[way, step, rows, :] = total.astype(jnp.bfloat16)
            self.copy(group, way, step).start()

    def result(self, group):
        last = NZ // 2 - 1
        rows = self.rows(group, 0, last)
        total = self.terms[self.p.z, rows, :]
        for way in range(2):
            self.copy(group, way, last).wait_recv()
            total += self.rbuf[way, last, rows, :].astype(jnp.float32)
        return total.astype(jnp.bfloat16)

    def finish(self, group):
        for way in range(2):
            for step in range(NZ // 2):
                self.copy(group, way, step).wait_send()


def weight_terms(group, abuf, gbuf, terms):
    begin, count = PARTS[group]
    rows = slice(begin, begin + count)
    width = terms.shape[2]
    per = WIDE // width

    def columns(n, carry):
        cols = pl.ds(pl.multiple_of(n * WIDE, WIDE), WIDE)
        acts = abuf[:, :, cols].reshape(gbuf.shape[1], WIDE)
        total = jnp.dot(gbuf[rows, :], acts, preferred_element_type=jnp.float32)
        for k in range(per):
            terms[n * per + k, rows, :] = total[:, k * width : (k + 1) * width]
        return carry

    lax.fori_loop(0, NZ // per, columns, 0)


class Span:
    def __init__(self, place, kbuf, vbuf, sends, recvs):
        self.p, self.bufs, self.sends, self.recvs = place, (kbuf, vbuf), sends, recvs

    def copy(self, which, hop):
        buf = self.bufs[which]
        source, target = (pl.ds(4, 2), pl.ds(2, 2)) if hop == 0 else (pl.ds(2, 2), pl.ds(0, 2))
        return remote(
            buf.at[source], buf.at[target], self.sends.at[which, hop], self.recvs.at[which, hop], self.p.at_c(1)
        )

    def finish(self):
        for which in range(2):
            for hop in range(2):
                self.copy(which, hop).wait_send()


class Return:
    def __init__(self, place, accs, sbuf, rbuf, sends, recvs):
        self.p, self.accs, self.sbuf, self.rbuf, self.sends, self.recvs = place, accs, sbuf, rbuf, sends, recvs

    def copy(self, which, hop):
        return remote(
            self.sbuf.at[which, hop],
            self.rbuf.at[which, hop],
            self.sends.at[which, hop],
            self.recvs.at[which, hop],
            self.p.at_c(-1),
        )

    def start(self, which, hop):
        if hop:
            self.copy(which, 0).wait_recv()
        for k in range(2):
            total = self.accs[which][2 * hop + k]
            if hop:
                total += self.rbuf[which, 0, k].astype(jnp.float32)
            self.sbuf[which, hop, k] = total.astype(jnp.bfloat16)
        self.copy(which, hop).start()

    def landed(self, which, factor, gbuf, row):
        self.copy(which, 1).wait_recv()
        for k in range(2):
            total = self.accs[which][4 + k] + self.rbuf[which, 1, k].astype(jnp.float32)
            gbuf[row : row + HEAD_SIZE, k * WIDE : (k + 1) * WIDE] = (total * factor).astype(jnp.bfloat16).T

    def finish(self):
        for which in range(2):
            for hop in range(2):
                self.copy(which, hop).wait_send()


def partners(place):
    others = [place.at_x(s) for s in (1, -1)] + [place.at_y(s) for s in (1, -1)]
    return others + [place.sibling(), place.at_c(1), place.at_c(-1)] + [place.at_z(1), place.at_z(-1)]


def doc_starts(docs, first, out):
    pos = first + lax.broadcasted_iota(jnp.int32, (1, out.shape[1]), 1)
    start = jnp.zeros_like(pos)
    end = jnp.int32(0)
    for n in range(docs.shape[0]):
        end = end + docs[n]
        start = jnp.where(pos >= end, end, start)
    out[...] = start


def near(qs):
    return slice(qs * WIDE, (qs + 1) * WIDE)


def reached(blocks):
    return [(qs, w, w - qs) for qs in range(2) for w in blocks if 0 <= w - qs < REACH]


def scores(h, blocks, base, starts, kbuf, qt, sc, top):
    row = lax.broadcasted_iota(jnp.int32, (WIDE, WIDE), 0)
    col = lax.broadcasted_iota(jnp.int32, (WIDE, WIDE), 1)
    tops = {}
    for qs, w, j in reached(blocks):
        s = jnp.dot(kbuf[w], qt[h, :, near(qs)], preferred_element_type=jnp.float32)
        seen = row >= starts[:, near(qs)] - (base + w * WIDE)
        if j == REACH - 1:
            seen &= row <= col
        s = jnp.where(seen, s, -jnp.inf)
        sc[h, qs, j] = s
        most = jnp.max(s, axis=0, keepdims=True)
        tops[qs] = jnp.maximum(tops[qs], most) if qs in tops else most
    for qs, most in tops.items():
        top[h, :, near(qs)] = jnp.maximum(top[h, :, near(qs)], most)


def value_products(h, blocks, vbuf, gt, dp):
    for qs, w, j in reached(blocks):
        dp[h, qs, j] = jnp.dot(vbuf[w], gt[h, :, near(qs)], preferred_element_type=jnp.float32)


def softmax(h, gh, sc, dp, top, inverse, mixed, dv):
    factor = HEAD_SIZE**-0.5 * math.log2(math.e)
    for qs in range(2):
        shift = top[h, :, near(qs)] * factor
        total = None
        for j in range(REACH):
            p = jnp.exp2(sc[h, qs, j] * factor - shift)
            sc[h, qs, j] = p
            part = jnp.sum(p, axis=0, keepdims=True)
            total = part if total is None else total + part
        inverse[h, :, near(qs)] = 1.0 / total
    for qs in range(2):
        scale = inverse[h, :, near(qs)]
        delta = None
        for j in range(REACH):
            p = sc[h, qs, j] * scale
            if qs + j >= 2:
                part = jnp.sum(p * dp[h, qs, j], axis=0, keepdims=True)
                delta = part if delta is None else delta + part
            dv[qs + j] += jnp.dot(p.astype(jnp.bfloat16), gh[h, near(qs)], preferred_element_type=jnp.float32)
        mixed[h, :, near(qs)] = delta


def score_grads(h, vbuf, kt, qh, gt, sc, dp, inverse, mixed, dk, gbuf):
    f32, bf16 = jnp.float32, jnp.bfloat16
    deltas = [mixed[h, :, near(qs)] for qs in range(2)]
    for qs, w, j in reached((0, 1)):
        d = jnp.dot(vbuf[w], gt[h, :, near(qs)], preferred_element_type=f32)
        dp[h, qs, j] = d
        deltas[qs] += jnp.sum(sc[h, qs, j] * inverse[h, :, near(qs)] * d, axis=0, keepdims=True)
    for qs in range(2):
        scale = inverse[h, :, near(qs)]
        dq = None
        for j in range(REACH):
            ds = (sc[h, qs, j] * scale * (dp[h, qs, j] - deltas[qs])).astype(bf16)
            dk[qs + j] += jnp.dot(ds, qh[h, near(qs)], preferred_element_type=f32)
            term = jnp.dot(kt[qs + j], ds, preferred_element_type=f32)
            dq = term if dq is None else dq + term
        rows = pl.ds(pl.multiple_of(h * HEAD_SIZE, HEAD_SIZE), HEAD_SIZE)
        gbuf[rows, near(qs)] = (dq * HEAD_SIZE**-0.5).astype(bf16)


def kernel(
    docs, act, q, k, v, g, out,
    abuf, relay, gbuf, terms, sbuf, rbuf, kbuf, vbuf, kt, qh, gh, qt, gt, sc, dp, dk, dv, starts, top, inverse, mixed,
    back_s, back_r, loads, local, as_, ar_, gs_, gr_, ss_, sr_, ks_, kr_, bs_, br_,
):
    place = Place()
    acts = Acts(place, act, abuf, relay, local, as_, ar_)
    gather = Gather(place, gbuf, gs_, gr_)
    scatter = Scatter(place, terms, sbuf, rbuf, ss_, sr_)
    span = Span(place, kbuf, vbuf, ks_, kr_)
    back = Return(place, (dk, dv), back_s, back_r, bs_, br_)
    heads, tokens = qh.shape[0], qh.shape[1]
    first = place.c * tokens
    base = first - SPAN * tokens
    barrier = pltpu.get_barrier_semaphore()
    others = partners(place)
    for other in others:
        pl.semaphore_signal(barrier, inc=1, device_id=other, device_id_type=MESH)
    copies = [
        pltpu.make_async_copy(k, kbuf.at[pl.ds(4, 2)], loads.at[0]),
        pltpu.make_async_copy(v, vbuf.at[pl.ds(4, 2)], loads.at[1]),
    ]
    for h in range(heads):
        cols = pl.ds(h * HEAD_SIZE, HEAD_SIZE)
        copies.append(pltpu.make_async_copy(q.at[:, cols], qh.at[h], loads.at[2 + 2 * h]))
        copies.append(pltpu.make_async_copy(g.at[:, cols], gh.at[h], loads.at[3 + 2 * h]))
    for copy in copies:
        copy.start()
    for copy in copies[:2]:
        copy.wait()
    pl.semaphore_wait(barrier, len(others))
    span.copy(0, 0).start()
    span.copy(1, 0).start()
    acts.own().start()
    doc_starts(docs, first, starts)
    dk[...] = jnp.zeros_like(dk)
    dv[...] = jnp.zeros_like(dv)
    top[...] = jnp.full_like(top, -jnp.inf)
    for copy in copies[2:]:
        copy.wait()

    def each_head(step):
        def body(h, carry):
            step(h)
            return carry

        lax.fori_loop(0, heads, body, 0)

    def turn(h):
        qt[h] = qh[h].T
        gt[h] = gh[h].T

    def own(h):
        scores(h, (4, 5), base, starts, kbuf, qt, sc, top)
        value_products(h, (4, 5), vbuf, gt, dp)

    def middle(h):
        scores(h, (2, 3), base, starts, kbuf, qt, sc, top)
        value_products(h, (2, 3), vbuf, gt, dp)

    def far(h):
        scores(h, (0, 1), base, starts, kbuf, qt, sc, top)
        softmax(h, gh, sc, dp, top, inverse, mixed, dv)

    def last(h):
        score_grads(h, vbuf, kt, qh, gt, sc, dp, inverse, mixed, dk, gbuf)

        @pl.when(h < 2)
        def _():
            gather.start(h)

    each_head(turn)
    span.copy(0, 0).wait_recv()
    span.copy(0, 1).start()
    acts.start()
    each_head(own)
    span.copy(1, 0).wait_recv()
    span.copy(1, 1).start()
    each_head(middle)
    for n in (2, 3, 4, 5):
        kt[n] = kbuf[n].T
    span.copy(0, 1).wait_recv()
    for n in (0, 1):
        kt[n] = kbuf[n].T
    each_head(far)
    back.start(1, 0)
    acts.forward()
    acts.spread(1)
    acts.spread(3)
    span.copy(1, 1).wait_recv()
    each_head(last)
    back.start(0, 0)
    back.start(1, 1)
    gather.start(2)
    gather.start(3)
    acts.spread(2)
    gather.forward(0)
    back.landed(1, 1.0, gbuf, 5 * HEAD_SIZE)
    gather.start(5)
    acts.spread_on(1)
    acts.spread_on(3)
    gather.forward(1)
    back.start(0, 1)
    gather.forward(2)
    acts.spread_on(2)
    acts.spread_last(1)
    acts.spread_last(3)
    gather.forward(3)
    back.landed(0, HEAD_SIZE**-0.5, gbuf, 4 * HEAD_SIZE)
    gather.start(4)
    acts.spread_last(2)
    gather.forward(5)
    gather.landed(0)
    gather.landed(1)
    acts.landed()
    gather.forward(4)
    weight_terms(0, abuf, gbuf, terms)
    scatter.step(0, 0)
    gather.landed(2)
    gather.landed(3)
    weight_terms(1, abuf, gbuf, terms)
    scatter.step(1, 0)
    scatter.step(0, 1)
    gather.landed(5)
    gather.landed(4)
    weight_terms(2, abuf, gbuf, terms)
    scatter.step(2, 0)
    scatter.step(1, 1)
    scatter.step(0, 2)
    scatter.step(2, 1)
    scatter.step(1, 2)
    scatter.step(0, 3)
    scatter.step(2, 2)
    scatter.step(1, 3)
    out[0:WIDE, :] = scatter.result(0)
    scatter.step(2, 3)
    out[WIDE : 2 * WIDE, :] = scatter.result(1)
    out[2 * WIDE : 3 * WIDE, :] = scatter.result(2)
    acts.finish()
    span.finish()
    back.finish()
    for n in range(heads + 2):
        gather.finish(n)
    for group in range(len(PARTS)):
        scatter.finish(group)


def turned(total, wq, wk, wv):
    columns = wq.shape[1]
    for n in range(columns // HEAD_SIZE):
        rows = slice(n * HEAD_SIZE, (n + 1) * HEAD_SIZE)
        wq[:, rows] = total[rows, :].T
    wk[...] = total[columns : columns + HEAD_SIZE, :].T
    wv[...] = total[columns + HEAD_SIZE : columns + 2 * HEAD_SIZE, :].T


def shards(doc_lengths, activations, queries, key_heads, head_values, output_gradient):
    tokens, features = activations.shape
    heads = queries.shape[1] // HEAD_SIZE
    quarter = features // NX
    chunk = quarter // NZ
    blocks = (SPAN + 1) * tokens // WIDE
    width = (heads + 2) * HEAD_SIZE
    bf16, f32 = jnp.bfloat16, jnp.float32
    dma = pltpu.SemaphoreType.DMA
    vmem = pl.BlockSpec(memory_space=pltpu.VMEM)
    total = pl.pallas_call(
        kernel,
        out_shape=jax.ShapeDtypeStruct((width, chunk), bf16),
        in_specs=[pl.BlockSpec(memory_space=pltpu.SMEM)] + [pl.BlockSpec(memory_space=pl.ANY)] * 5,
        out_specs=vmem,
        scratch_shapes=[
            pltpu.VMEM((NX, tokens, quarter), bf16),
            pltpu.VMEM((2, tokens // (2 * NY * NCORE), quarter), bf16),
            pltpu.VMEM((width, NX * tokens), bf16),
            pltpu.VMEM((NZ, width, chunk), f32),
            pltpu.VMEM((2, NZ // 2, width, chunk), bf16),
            pltpu.VMEM((2, NZ // 2, width, chunk), bf16),
            pltpu.VMEM((blocks, WIDE, HEAD_SIZE), bf16),
            pltpu.VMEM((blocks, WIDE, HEAD_SIZE), bf16),
            pltpu.VMEM((blocks, HEAD_SIZE, WIDE), bf16),
            pltpu.VMEM((heads, tokens, HEAD_SIZE), bf16),
            pltpu.VMEM((heads, tokens, HEAD_SIZE), bf16),
            pltpu.VMEM((heads, HEAD_SIZE, tokens), bf16),
            pltpu.VMEM((heads, HEAD_SIZE, tokens), bf16),
            pltpu.VMEM((heads, 2, REACH, WIDE, WIDE), f32),
            pltpu.VMEM((heads, 2, REACH, WIDE, WIDE), f32),
            pltpu.VMEM((blocks, WIDE, HEAD_SIZE), f32),
            pltpu.VMEM((blocks, WIDE, HEAD_SIZE), f32),
            pltpu.VMEM((1, tokens), jnp.int32),
            pltpu.VMEM((heads, 1, tokens), f32),
            pltpu.VMEM((heads, 1, tokens), f32),
            pltpu.VMEM((heads, 1, tokens), f32),
            pltpu.VMEM((2, 2, 2, WIDE, HEAD_SIZE), bf16),
            pltpu.VMEM((2, 2, 2, WIDE, HEAD_SIZE), bf16),
            dma((2 + 2 * heads,)),
            dma,
            dma((8 * NX,)),
            dma((8 * NX,)),
            dma((heads + 2, 4)),
            dma((heads + 2, 4)),
            dma((len(PARTS), 2, NZ // 2)),
            dma((len(PARTS), 2, NZ // 2)),
            dma((2, 2)),
            dma((2, 2)),
            dma((2, 2)),
            dma((2, 2)),
        ],
        compiler_params=pltpu.CompilerParams(
            collective_id=0, has_side_effects=True, vmem_limit_bytes=56 * 2**20
        ),
    )(
        doc_lengths,
        activations,
        queries,
        key_heads.reshape(-1, WIDE, HEAD_SIZE),
        head_values.reshape(-1, WIDE, HEAD_SIZE),
        output_gradient,
    )
    return pl.pallas_call(
        turned,
        out_shape=(
            jax.ShapeDtypeStruct((chunk, heads * HEAD_SIZE), bf16),
            jax.ShapeDtypeStruct((chunk, HEAD_SIZE), bf16),
            jax.ShapeDtypeStruct((chunk, HEAD_SIZE), bf16),
        ),
        in_specs=[vmem],
        out_specs=[vmem] * 3,
    )(total)


def solution(mesh):
    return jax.shard_map(
        shards,
        mesh=mesh,
        in_specs=(
            P(),
            P("ctx", None),
            P("ctx", "tp"),
            P("ctx", "tp"),
            P("ctx", "tp"),
            P("ctx", "tp"),
        ),
        out_specs=(P("ctx", "tp"), P("ctx", "tp"), P("ctx", "tp")),
        check_vma=False,
    )
```
